128 devices in a mesh: box: 4 (over z_hi, core), samp: 32 (over z_lo, y, x).
Axes of the slice: x: 4, y: 4, z: 4 (z_hi: 2, z_lo: 2; z = z_hi * 2 + z_lo), core: 2. Of those that a mesh axis runs over, the one named last changes fastest.
Arguments:
- child_out: float32 [4096, 2, 18432], P(('box', 'samp')), may hold values from -6 to 6
- child_octant: int32 [512, 8], P(('box', 'samp')), may hold values from 0 to 7, each once within a row
- theta_index: int32 [192, 4], replicated, may hold values from 0 to 95, as said below
- theta_weight: float32 [192, 4], replicated, may hold values from -0.2 to 0.6
- phi_index: int32 [384, 4], replicated, may hold values from 0 to 191, as said below
- phi_weight: float32 [384, 4], replicated, may hold values from -0.2 to 0.6
- shift_angle: float32 [8, 192, 384], replicated, may hold values from -3.140625 to 3.140625
- partner_src: int32 [512, 32], replicated, may hold values from 0 to 511
- partner_disp: int32 [512, 32], replicated, may hold values from 0 to 315
- translation: float32 [316, 2, 192, 384], P(None, None, 'samp'), may hold values from -0.75 to 0.75
Outputs:
- child_in: float32 [4096, 2, 18432], P(('box', 'samp'))
The draws below stay inside these ranges and needn't reach their ends.
Inputs may be any that keep to these rules, and one draw needn't show every extreme that they name: `theta_index`: four stencil indices for each fine theta sample, consecutive coarse samples near it, clipped to the ends so that they may repeat near the poles (repeated weights add). `phi_index`: four consecutive coarse phi samples near each fine phi sample, wrapping around in phi.
All inputs are finite; a program needn't handle non-finite values.
Results may differ from the reference program's by a relative error of at most 0.00007.
Values sent between devices are 32-bit elements; how exact they have to be, the bound alone decides.
No kernel may reach another device: no remote copies, remote signals or barrier semaphores. Data moves between devices by JAX's collectives and lax.ppermute only.
A program may use at most 256 MiB of HBM per device.

```python
import jax
import jax.numpy as jnp
from jax import lax

NT1 = 96
NP1 = 192
NT2 = 192
NP2 = 384
NDISP = 316
NPART = 32
NB1 = 4096
NB2 = 512


def draw_theta_index(key, part):
    rows = jnp.arange(NT2, dtype=jnp.int32)
    offset = jax.random.randint(key, (NT2, 1), 0, 3, dtype=jnp.int32)
    start = (rows * NT1 // NT2)[:, None] - 2 + offset
    return jnp.clip(start + jnp.arange(4, dtype=jnp.int32)[None, :], 0, NT1 - 1).astype(jnp.int32)


def draw_phi_index(key, part):
    rows = jnp.arange(NP2, dtype=jnp.int32)
    offset = jax.random.randint(key, (NP2, 1), 0, 3, dtype=jnp.int32)
    start = (rows * NP1 // NP2)[:, None] - 2 + offset
    return jnp.mod(start + jnp.arange(4, dtype=jnp.int32)[None, :], NP1).astype(jnp.int32)


def place_ends(values, own_key, smallest, largest):
    dims = values.shape
    spot = [jax.random.randint(jax.random.fold_in(own_key, axis), (), 0, dims[axis]) for axis in range(len(dims))]
    values = values.at[tuple(spot)].set(smallest)
    longest = dims.index(max(dims))
    spot[longest] = (spot[longest] + 1) % dims[longest]
    return values.at[tuple(spot)].set(largest)


def level_of(key, dims, pieces, low, top_value):
    loudness = 1.0
    for dim, blocks in pieces:
        heights = jax.random.uniform(jax.random.fold_in(jax.random.fold_in(key, 6), dim), (blocks,), jnp.float32, low / len(pieces), top_value / len(pieces))
        loudness = loudness * jnp.repeat(jnp.exp(heights), dims[dim] // blocks).reshape((-1,) + (1,) * (len(dims) - 1 - dim))
    return loudness


def gaussian(key, extent, deviation, reach, pieces=(), kind=jnp.bfloat16):
    level = level_of(key, extent, pieces, -0.22, 0.18) if pieces else 1.0
    entries = jax.random.normal(key, extent, jnp.float32) * deviation * level
    return jnp.minimum(jnp.maximum(entries, -reach), reach).astype(kind)


def setup_inputs(seed: int = 0) -> dict:
    arg_keys = jax.random.split(jax.random.key(seed), 11)
    child_out = gaussian(arg_keys[0], (NB1, 2, NT1 * NP1), 1.0, 6.0, ((0, 128),), jnp.float32)
    child_octant = jax.vmap(lambda own: jax.random.permutation(own, 8))(jax.random.split(arg_keys[1], NB2)).reshape((NB2, 8)).astype(jnp.int32)
    theta_index = draw_theta_index(jax.random.fold_in(arg_keys[10], 71), 0)
    theta_weight = jnp.clip(jax.random.uniform(arg_keys[3], (NT2, 4), jnp.float32, -0.2, 0.6), -0.2, 0.6)
    phi_index = draw_phi_index(jax.random.fold_in(arg_keys[10], 71), 0)
    phi_weight = jnp.clip(jax.random.uniform(arg_keys[5], (NP2, 4), jnp.float32, -0.2, 0.6), -0.2, 0.6)
    shift_angle = jnp.clip(jax.random.uniform(arg_keys[6], (8, NT2, NP2), jnp.float32, -3.140625, 3.140625), -3.140625, 3.140625)
    partner_src = place_ends(jax.random.randint(arg_keys[7], (NB2, NPART), 0, NB2), jax.random.fold_in(arg_keys[7], 1), 0, NB2 - 1).astype(jnp.int32)
    partner_disp = place_ends(jax.random.randint(arg_keys[8], (NB2, NPART), 0, NDISP), jax.random.fold_in(arg_keys[8], 1), 0, NDISP - 1).astype(jnp.int32)
    translation = gaussian(arg_keys[9], (NDISP, 2, NT2, NP2), (1.0 / (2 * NPART) ** 0.5), 0.75, ((2, 32),), jnp.float32)
    return dict(child_out=child_out, child_octant=child_octant, theta_index=theta_index, theta_weight=theta_weight, phi_index=phi_index, phi_weight=phi_weight, shift_angle=shift_angle, partner_src=partner_src, partner_disp=partner_disp, translation=translation)


PRECISE = lax.Precision.HIGHEST


def stencil(index, weight, count):
    hits = (index[:, :, None] == jnp.arange(count, dtype=jnp.int32)[None, None, :]).astype(weight.dtype)
    return jnp.sum(weight[:, :, None] * hits, axis=1)


def spread(field, theta_mat, phi_mat):
    wider = jnp.einsum("czap,qp->czaq", field, phi_mat, precision=PRECISE)
    return jnp.einsum("ta,czaq->cztq", theta_mat, wider, precision=PRECISE)


def contract(field, theta_mat, phi_mat):
    narrow = jnp.einsum("ta,cztq->czaq", theta_mat, field, precision=PRECISE)
    return jnp.einsum("czaq,qp->czap", narrow, phi_mat, precision=PRECISE)


def rotate(field, cosine, sine_part):
    real_part = field[:, 0]
    imag_part = field[:, 1]
    return jnp.stack([real_part * cosine - imag_part * sine_part, real_part * sine_part + imag_part * cosine], axis=1)


def rotate_back(field, cosine, sine_part):
    real_part = field[:, 0]
    imag_part = field[:, 1]
    return jnp.stack([real_part * cosine + imag_part * sine_part, imag_part * cosine - real_part * sine_part], axis=1)


def reference(child_out, child_octant, theta_index, theta_weight, phi_index, phi_weight, shift_angle, partner_src, partner_disp, translation):
    theta_mat = stencil(theta_index, theta_weight, NT1)
    phi_mat = stencil(phi_index, phi_weight, NP1)
    cos_table = jnp.cos(shift_angle)
    sin_table = jnp.sin(shift_angle)
    children = child_out.reshape(NB2, 8, 2, NT1, NP1)

    def aggregate(items):
        kids, octants = items
        cos_sel = jnp.take(cos_table, octants, axis=0)
        sin_sel = jnp.take(sin_table, octants, axis=0)
        fine_child = rotate(spread(kids, theta_mat, phi_mat), cos_sel, sin_sel)
        return jnp.sum(fine_child, axis=0)

    parent_out = lax.map(aggregate, (children, child_octant))

    def translate_one(items):
        sources, displacements = items
        picked = jnp.take(parent_out, sources, axis=0)
        operators = jnp.take(translation, displacements, axis=0)
        real_sum = jnp.sum(operators[:, 0] * picked[:, 0] - operators[:, 1] * picked[:, 1], axis=0)
        imag_sum = jnp.sum(operators[:, 0] * picked[:, 1] + operators[:, 1] * picked[:, 0], axis=0)
        return jnp.stack([real_sum, imag_sum], axis=0)

    parent_in = lax.map(translate_one, (partner_src, partner_disp))

    def disaggregate(items):
        parent, octants = items
        cos_sel = jnp.take(cos_table, octants, axis=0)
        sin_sel = jnp.take(sin_table, octants, axis=0)
        repeated = jnp.broadcast_to(parent[None], (8,) + parent.shape)
        return contract(rotate_back(repeated, cos_sel, sin_sel), theta_mat, phi_mat)

    child_in = lax.map(disaggregate, (parent_in, child_octant))
    return child_in.reshape(NB1, 2, NT1 * NP1)
```

```python
import functools

import jax
import jax.numpy as jnp
import numpy as np
from jax import lax
from jax.experimental import pallas as pl
from jax.experimental.pallas import tpu as pltpu
from jax.sharding import Mesh, PartitionSpec as P

NT1, NP1, NT2, NP2 = 96, 192, 192, 384
NDISP, NPART = 316, 32
CHIPS = 64
PARENTS = 4
ROWS = 72
F32, BF16 = jnp.float32, jnp.bfloat16
ALL = ("zh", "c", "zl", "y", "x")
CHIP = ("zh", "zl", "y", "x")


def fit(fn, powers):
    h = 0.7855 * (1 - np.cos(np.pi * (np.arange(400) + 0.5) / 400))
    a = np.stack([h**k for k in powers], 1)
    return [float(v) for v in np.linalg.lstsq(a, fn(h), rcond=None)[0]]


SIN = fit(np.sin, (1, 3, 5, 7, 9, 11))
COS = fit(np.cos, (0, 2, 4, 6, 8, 10))


def horner(z, coefs):
    r = jnp.full_like(z, coefs[-1])
    for c in coefs[-2::-1]:
        r = r * z + c
    return r


def split(x):
    hi = x.astype(BF16)
    return hi, (x - hi.astype(F32)).astype(BF16)


def dot(a, b):
    return jnp.dot(a, b, preferred_element_type=F32)


def stencil_t(index, weight, rows, target):
    n = index.shape[1]
    row = lax.broadcasted_iota(jnp.int32, (rows, n), 0)
    out = jnp.zeros((rows, n), F32)
    for j in range(4):
        out = out + jnp.where(row == target(index[j : j + 1, :]), weight[j : j + 1, :], 0.0)
    return out


def even_odd(a):
    return jnp.where(a % 2 == 0, a // 2, 48 + a // 2)


def unit_row(p, u, part):
    return p * 16 + part * 8 + u if u < 8 else 64 + 2 * p + part


def aggregate_kernel(
    oct_ref, x_ref, angle_ref, ti_ref, tw_ref, pi_ref, pw_ref,
    out_ref, cos_ref, sin_ref,
    t3_ref, pe_ref, po_ref, vh_ref, vl_ref, y3_ref, acc_ref,
):
    p = pl.program_id(0)

    @pl.when(p == 0)
    def _():
        def trig(o, _):
            for r in range(0, NT2, 48):
                h = angle_ref[o, r : r + 48, :] * 0.5
                z = h * h
                s = horner(z, SIN) * h
                c = horner(z, COS)
                cos_ref[o, r : r + 48, :] = 1.0 - 2.0 * (s * s)
                sin_ref[o, r : r + 48, :] = 2.0 * (s * c)
            return 0

        lax.fori_loop(0, 8, trig, 0)
        tt = stencil_t(ti_ref[...], tw_ref[...], 128, even_odd)
        t = jnp.transpose(jnp.concatenate([tt, jnp.zeros((128, 64), F32)], axis=1))[:NT2, :NT1]
        hi, lo = split(t)
        t3_ref[...] = jnp.concatenate([hi, hi, lo], axis=1)
        for ref, shift in ((pe_ref, 0), (po_ref, 64)):
            hi, lo = split(stencil_t(pi_ref[...], pw_ref[...], 256, lambda a: a + shift))
            ref[0], ref[1] = hi, lo

    for k in range(8):
        for part in range(2):
            row = (k * 2 + part) * 48
            for tile in range(3):
                v = x_ref[pl.ds(k * 288 + 2 * tile + part, 48, stride=6), :]
                hi, lo = split(v)
                vh_ref[row : row + 48, tile * 128 : tile * 128 + 128] = hi
                vl_ref[row : row + 48, tile * 128 : tile * 128 + 128] = lo
    for odd, ref in ((0, pe_ref), (1, po_ref)):
        cols = slice(odd * 128, odd * 128 + 256)
        for m in range(0, 768, 192):
            vh, vl = vh_ref[m : m + 192, cols], vl_ref[m : m + 192, cols]
            y = dot(vh, ref[0]) + dot(vl, ref[0]) + dot(vh, ref[1])
            yh, yl = split(y)
            for kk in range(2):
                for part in range(2):
                    r = (kk * 2 + part) * 48
                    for j in range(3):
                        col = j * 256 + part * 128
                        for base, v in ((0, yh), (96, yl), (192, yh)):
                            y3_ref[m // 96 + kk, base + odd * 48 : base + odd * 48 + 48, col : col + 128] = v[
                                r : r + 48, j * 128 : j * 128 + 128
                            ]

    acc_ref[...] = jnp.zeros_like(acc_ref)

    def child(k, _):
        o = oct_ref[p, k]
        for j in range(3):
            f = dot(t3_ref[...], y3_ref[k, :, j * 256 : j * 256 + 256])
            re, im = f[:, :128], f[:, 128:]
            c = cos_ref[o, :, j * 128 : j * 128 + 128]
            s = sin_ref[o, :, j * 128 : j * 128 + 128]
            acc_ref[2 * j] += re * c - im * s
            acc_ref[2 * j + 1] += re * s + im * c
        return 0

    lax.fori_loop(0, 8, child, 0)
    for part in range(2):
        for j in range(3):
            for r in range(3):
                u = r * 3 + j
                base = p * 16 + part * 8 + u if u < 8 else 64 + 2 * p + part
                for zh in range(2):
                    v = acc_ref[2 * j + part, pl.ds(3 * zh + r, 32, stride=6), :]
                    out_ref[pl.ds(zh * 32 * ROWS + base, 32, stride=ROWS), :] = v


def operators_kernel(zh_ref, t_ref, out_ref):
    half = zh_ref[0] * 18

    def one(d, _):
        base = d * 36 + half
        to = pl.multiple_of(d * 24, 8)
        out_ref[pl.ds(to, 8), :] = t_ref[pl.ds(base, 8, stride=2), :]
        out_ref[pl.ds(to + 8, 8), :] = t_ref[pl.ds(base + 1, 8, stride=2), :]
        last = t_ref[pl.ds(base + 16, 2), :]
        out_ref[pl.ds(to + 16, 8), :] = jnp.concatenate([last, last, last, last], axis=0)
        return 0

    lax.fori_loop(0, NDISP, one, 0, unroll=4)


def translate_kernel(src_ref, left_ref, disp_ref, own_ref, other_ref, t_ref, out_ref, s_ref, l_ref, sem):
    n = CHIPS * ROWS
    copies = [
        pltpu.make_async_copy(own_ref, s_ref.at[pl.ds(0, n)], sem.at[0]),
        pltpu.make_async_copy(other_ref, s_ref.at[pl.ds(n, n)], sem.at[1]),
    ]
    for c in copies:
        c.start()
    for c in copies:
        c.wait()

    def spread(i, _):
        v = s_ref[pl.ds(pl.multiple_of(i * ROWS + 64, 8), 8), :]
        for p in range(PARENTS):
            re, im = v[2 * p : 2 * p + 1], v[2 * p + 1 : 2 * p + 2]
            four = jnp.concatenate([re, im, im, re], axis=0)
            l_ref[pl.ds(pl.multiple_of((i * 4 + p) * 8, 8), 8), :] = jnp.concatenate([four, four], axis=0)
        return 0

    lax.fori_loop(0, 2 * CHIPS, spread, 0, unroll=2)

    def receiver(i, _):
        rr = ii = ri = ir = left = None
        for q in range(NPART):
            at = i * NPART + q
            a = pl.multiple_of(src_ref[at], 8)
            b = pl.multiple_of(left_ref[at], 8)
            d = pl.multiple_of(disp_ref[at], 8)
            sr, si = s_ref[pl.ds(a, 8), :], s_ref[pl.ds(a + 8, 8), :]
            tr, ti = t_ref[pl.ds(d, 8), :], t_ref[pl.ds(d + 8, 8), :]
            terms = (tr * sr, ti * si, tr * si, ti * sr, t_ref[pl.ds(d + 16, 8), :] * l_ref[pl.ds(b, 8), :])
            if q == 0:
                rr, ii, ri, ir, left = terms
            else:
                rr, ii, ri, ir, left = rr + terms[0], ii + terms[1], ri + terms[2], ir + terms[3], left + terms[4]
        chip, p = i // PARENTS, i % PARENTS
        base = chip * ROWS
        to = pl.multiple_of(base + p * 16, 8)
        out_ref[pl.ds(to, 8), :] = rr - ii
        out_ref[pl.ds(to + 8, 8), :] = ri + ir
        ends = jnp.concatenate([left[0:1] - left[1:2], left[2:3] + left[3:4]], axis=0)
        out_ref[pl.ds(base + 64 + 2 * p, 2), :] = ends
        return 0

    lax.fori_loop(0, CHIPS * PARENTS, receiver, 0)


def disaggregate_kernel(
    oct_ref, x_ref, cos_ref, sin_ref, ti_ref, tw_ref, pi_ref, pw_ref,
    out_ref,
    t_ref, pe_ref, po_ref, in_ref, r3_ref, z3_ref,
):
    p = pl.program_id(0)

    @pl.when(p == 0)
    def _():
        hi, lo = split(stencil_t(ti_ref[...], tw_ref[...], NT1, even_odd))
        t_ref[...] = jnp.concatenate([hi, hi, lo], axis=1)
        for ref, shift in ((pe_ref, 0), (po_ref, 64)):
            m = jnp.transpose(stencil_t(pi_ref[...], pw_ref[...], 256, lambda a: a + shift))
            hi, lo = split(m)
            ref[...] = jnp.concatenate([hi, hi, lo], axis=0)

    for part in range(2):
        for j in range(3):
            for r in range(3):
                u = r * 3 + j
                base = p * 16 + part * 8 + u if u < 8 else 64 + 2 * p + part
                for zh in range(2):
                    v = x_ref[pl.ds(zh * 32 * ROWS + base, 32, stride=ROWS), :]
                    in_ref[2 * j + part, pl.ds(3 * zh + r, 32, stride=6), :] = v

    def child(k, _):
        o = oct_ref[p, k]
        for j in range(3):
            re, im = in_ref[2 * j], in_ref[2 * j + 1]
            c = cos_ref[o, :, j * 128 : j * 128 + 128]
            s = sin_ref[o, :, j * 128 : j * 128 + 128]
            for part, v in ((0, re * c + im * s), (1, im * c - re * s)):
                hi, lo = split(v)
                cols = slice(part * 128, part * 128 + 128)
                r3_ref[j, 0:192, cols] = hi
                r3_ref[j, 192:384, cols] = lo
                r3_ref[j, 384:576, cols] = hi
            z = dot(t_ref[...], r3_ref[j])
            hi, lo = split(z)
            for part in range(2):
                for odd in range(2):
                    for base, v in ((0, hi), (384, lo), (768, hi)):
                        row = pl.multiple_of((k * 2 + part) * 48, 16)
                        z3_ref[odd, pl.ds(row, 48), base + j * 128 : base + j * 128 + 128] = v[
                            odd * 48 : odd * 48 + 48, part * 128 : part * 128 + 128
                        ]
        return 0

    lax.fori_loop(0, 8, child, 0)
    for k in range(8):
        rows = slice(k * 96, k * 96 + 96)
        even = dot(z3_ref[0, rows, :], pe_ref[...])
        odd = dot(z3_ref[1, rows, :], po_ref[...])
        tiles = (even[:, :128], even[:, 128:] + odd[:, :128], odd[:, 128:])
        for part in range(2):
            for tile in range(3):
                out_ref[pl.ds(k * 288 + 2 * tile + part, 48, stride=6), :] = tiles[tile][part * 48 : part * 48 + 48]


def whole(shape):
    return pl.BlockSpec(shape, lambda *_: (0,) * len(shape))


SMEM = pl.BlockSpec(memory_space=pltpu.SMEM)
LIMIT = 60 * 2**20


def local(
    child_out, child_octant, theta_index, theta_weight, phi_index, phi_weight,
    shift_angle, partner_src, partner_disp, translation,
):
    core = lax.axis_index("c")
    zh = lax.axis_index("zh")
    x = child_out.reshape(32, 2, 144, 128).transpose(0, 2, 1, 3).reshape(32 * 288, 128)
    stencils = (theta_index.T, theta_weight.T, phi_index.T, phi_weight.T)
    stencil_specs = [whole((4, NT2)), whole((4, NT2)), whole((4, NP2)), whole((4, NP2))]
    table = (8, NT2, NP2)
    rows = CHIPS * ROWS
    out, cosine, sine = pl.pallas_call(
        aggregate_kernel,
        grid=(PARENTS,),
        in_specs=[SMEM, pl.BlockSpec((8 * 288, 128), lambda p: (p, 0)), whole(table), *stencil_specs],
        out_specs=[whole((rows, 128)), whole(table), whole(table)],
        out_shape=[
            jax.ShapeDtypeStruct((rows, 128), F32),
            jax.ShapeDtypeStruct(table, F32),
            jax.ShapeDtypeStruct(table, F32),
        ],
        scratch_shapes=[
            pltpu.VMEM((NT2, 288), BF16),
            pltpu.VMEM((2, 256, NP2), BF16),
            pltpu.VMEM((2, 256, NP2), BF16),
            pltpu.VMEM((768, 384), BF16),
            pltpu.VMEM((768, 384), BF16),
            pltpu.VMEM((8, 288, 768), BF16),
            pltpu.VMEM((6, NT2, 128), F32),
        ],
        compiler_params=pltpu.CompilerParams(vmem_limit_bytes=LIMIT),
        cost_estimate=pl.CostEstimate(flops=8 * 10**9, bytes_accessed=14 * 10**6, transcendentals=0),
        name="aggregate",
    )(child_octant, x, shift_angle, *stencils)

    got = lax.all_to_all(out.reshape(CHIPS, ROWS, 128), CHIP, 0, 0, tiled=True).reshape(rows, 128)
    other = lax.ppermute(got, "c", [(0, 1), (1, 0)])

    operators = translation.reshape(NDISP, 2, 6, 3, 128).transpose(0, 2, 3, 1, 4).reshape(NDISP * 36, 128)
    operators = pl.pallas_call(
        operators_kernel,
        in_specs=[SMEM, pl.BlockSpec(memory_space=pltpu.VMEM)],
        out_specs=pl.BlockSpec(memory_space=pltpu.VMEM),
        out_shape=jax.ShapeDtypeStruct((NDISP * 24, 128), F32),
        compiler_params=pltpu.CompilerParams(vmem_limit_bytes=LIMIT),
        cost_estimate=pl.CostEstimate(flops=10**6, bytes_accessed=10**7, transcendentals=0),
        name="operators",
    )(zh.reshape(1), operators)

    def mine(a):
        return lax.dynamic_index_in_dim(a.reshape(2, 2, 128, NPART), core, 1, keepdims=False).reshape(-1)

    src = mine(partner_src)
    holder, p = src // 4, src % 4
    far = jnp.where((holder // 32) % 2 == core, 0, 1)
    chip = far * CHIPS + (holder // 64) * 32 + holder % 32
    src_at = chip * ROWS + p * 16
    left_at = (chip * 4 + p) * 8
    disp_at = mine(partner_disp) * 24
    hbm = pl.BlockSpec(memory_space=pl.ANY)
    incoming = pl.pallas_call(
        translate_kernel,
        in_specs=[SMEM, SMEM, SMEM, hbm, hbm, pl.BlockSpec(memory_space=pltpu.VMEM)],
        out_specs=pl.BlockSpec(memory_space=pltpu.VMEM),
        out_shape=jax.ShapeDtypeStruct((rows, 128), F32),
        scratch_shapes=[
            pltpu.VMEM((2 * rows, 128), F32),
            pltpu.VMEM((512 * 8, 128), F32),
            pltpu.SemaphoreType.DMA((2,)),
        ],
        compiler_params=pltpu.CompilerParams(vmem_limit_bytes=LIMIT),
        cost_estimate=pl.CostEstimate(flops=10**8, bytes_accessed=12 * 10**6, transcendentals=0),
        name="translate",
    )(src_at, left_at, disp_at, got, other, operators)

    back = lax.all_to_all(incoming.reshape(CHIPS, ROWS, 128), CHIP, 0, 0, tiled=True).reshape(rows, 128)
    y = pl.pallas_call(
        disaggregate_kernel,
        grid=(PARENTS,),
        in_specs=[SMEM, whole((rows, 128)), whole(table), whole(table), *stencil_specs],
        out_specs=pl.BlockSpec((8 * 288, 128), lambda p: (p, 0)),
        out_shape=jax.ShapeDtypeStruct((32 * 288, 128), F32),
        scratch_shapes=[
            pltpu.VMEM((NT1, 576), BF16),
            pltpu.VMEM((1152, 256), BF16),
            pltpu.VMEM((1152, 256), BF16),
            pltpu.VMEM((6, NT2, 128), F32),
            pltpu.VMEM((3, 576, 256), BF16),
            pltpu.VMEM((2, 768, 1152), BF16),
        ],
        compiler_params=pltpu.CompilerParams(vmem_limit_bytes=LIMIT),
        cost_estimate=pl.CostEstimate(flops=8 * 10**9, bytes_accessed=14 * 10**6, transcendentals=0),
        name="disaggregate",
    )(child_octant, back, cosine, sine, *stencils)
    return y.reshape(32, 144, 2, 128).transpose(0, 2, 1, 3).reshape(32, 2, NT1 * NP1)


def solution(mesh):
    fine = Mesh(mesh.devices.reshape(2, 2, 2, 4, 4), ALL)
    boxes = P(ALL)
    in_specs = (boxes, boxes, P(), P(), P(), P(), P(), P(), P(), P(None, None, ("zl", "y", "x"), None))
    return jax.shard_map(local, mesh=fine, in_specs=in_specs, out_specs=boxes, check_vma=False)
```

```python
import functools

import jax
import jax.numpy as jnp
import numpy as np
from jax import lax
from jax.experimental import pallas as pl
from jax.experimental.pallas import tpu as pltpu
from jax.sharding import Mesh, PartitionSpec as P

NT1, NP1, NT2, NP2 = 96, 192, 192, 384
NDISP, NPART = 316, 32
CHIPS = 64
PARENTS = 4
FIRST, SECOND = (0, 1), (2,)
F32, BF16 = jnp.float32, jnp.bfloat16
ALL = ("zh", "c", "zl", "y", "x")
CHIP = ("zh", "zl", "y", "x")


def fit(fn, powers):
    h = 0.7855 * (1 - np.cos(np.pi * (np.arange(400) + 0.5) / 400))
    a = np.stack([h**k for k in powers], 1)
    return [float(v) for v in np.linalg.lstsq(a, fn(h), rcond=None)[0]]


SIN = fit(np.sin, (1, 3, 5, 7, 9, 11))
COS = fit(np.cos, (0, 2, 4, 6, 8, 10))


def horner(z, coefs):
    r = jnp.full_like(z, coefs[-1])
    for c in coefs[-2::-1]:
        r = r * z + c
    return r


def split(x):
    hi = x.astype(BF16)
    return hi, (x - hi.astype(F32)).astype(BF16)


def dot(a, b):
    return jnp.dot(a, b, preferred_element_type=F32)


def stencil_t(index, weight, rows, target):
    n = index.shape[1]
    row = lax.broadcasted_iota(jnp.int32, (rows, n), 0)
    out = jnp.zeros((rows, n), F32)
    for j in range(4):
        out = out + jnp.where(row == target(index[j : j + 1, :]), weight[j : j + 1, :], 0.0)
    return out


def even_odd(a):
    return jnp.where(a % 2 == 0, a // 2, 48 + a // 2)


def shape_of(tiles):
    n = len(tiles)
    return n, 3 * n, 6 * n, 24 * n


def aggregate_kernel(tiles, tables, oct_ref, x_ref, angle_ref, ti_ref, tw_ref, pi_ref, pw_ref, out_ref, cos_ref, sin_ref, *scratch):
    t3_ref, pe_ref, po_ref, vh_ref, vl_ref, y3_ref, acc_ref = scratch
    n, half, box, rows = shape_of(tiles)
    p = pl.program_id(0)
    first = tiles[0] if tables else 0
    columns = slice(tiles[0] * 128, tiles[0] * 128 + n * 128)

    @pl.when(p == 0)
    def _():
        def trig(o, _):
            for r in range(0, NT2, 48):
                h = angle_ref[o, r : r + 48, :] * 0.5
                z = h * h
                s = horner(z, SIN) * h
                c = horner(z, COS)
                cos_ref[o, r : r + 48, :] = 1.0 - 2.0 * (s * s)
                sin_ref[o, r : r + 48, :] = 2.0 * (s * c)
            return 0

        lax.fori_loop(0, 8, trig, 0)
        tt = stencil_t(ti_ref[...], tw_ref[...], 128, even_odd)
        t = jnp.transpose(jnp.concatenate([tt, jnp.zeros((128, 64), F32)], axis=1))[:NT2, :NT1]
        hi, lo = split(t)
        t3_ref[...] = jnp.concatenate([hi, hi, lo], axis=1)
        for ref, shift in ((pe_ref, 0), (po_ref, 64)):
            hi, lo = split(stencil_t(pi_ref[:, columns], pw_ref[:, columns], 256, lambda a: a + shift))
            ref[0], ref[1] = hi, lo

    for k in range(8):
        for part in range(2):
            row = (k * 2 + part) * 48
            for tile in range(3):
                v = x_ref[pl.ds(k * 288 + 2 * tile + part, 48, stride=6), :]
                hi, lo = split(v)
                vh_ref[row : row + 48, tile * 128 : tile * 128 + 128] = hi
                vl_ref[row : row + 48, tile * 128 : tile * 128 + 128] = lo
    for odd, ref in ((0, pe_ref), (1, po_ref)):
        cols = slice(odd * 128, odd * 128 + 256)
        for m in range(0, 768, 192):
            vh, vl = vh_ref[m : m + 192, cols], vl_ref[m : m + 192, cols]
            y = dot(vh, ref[0]) + dot(vl, ref[0]) + dot(vh, ref[1])
            yh, yl = split(y)
            for kk in range(2):
                for part in range(2):
                    r = (kk * 2 + part) * 48
                    for j in range(n):
                        col = j * 256 + part * 128
                        for base, v in ((0, yh), (96, yl), (192, yh)):
                            y3_ref[m // 96 + kk, base + odd * 48 : base + odd * 48 + 48, col : col + 128] = v[
                                r : r + 48, j * 128 : j * 128 + 128
                            ]

    for k in range(8):
        o = oct_ref[p, k]
        for j in range(n):
            f = dot(t3_ref[...], y3_ref[k, :, j * 256 : j * 256 + 256])
            re, im = f[:, :128], f[:, 128:]
            at = (first + j) * 128
            c = cos_ref[o, :, at : at + 128]
            s = sin_ref[o, :, at : at + 128]
            if k == 0:
                acc_ref[2 * j] = re * c - im * s
                acc_ref[2 * j + 1] = re * s + im * c
            else:
                acc_ref[2 * j] += re * c - im * s
                acc_ref[2 * j + 1] += re * s + im * c

    for part in range(2):
        for j in range(n):
            for r in range(3):
                base = p * box + part * half + j * 3 + r
                for zh in range(2):
                    v = acc_ref[2 * j + part, pl.ds(3 * zh + r, 32, stride=6), :]
                    out_ref[pl.ds(zh * 32 * rows + base, 32, stride=rows), :] = v


def operators_kernel(zh_ref, t_ref, first_ref, second_ref):
    half = zh_ref[0] * 18

    def one(d, _):
        for ref, tiles, slots in ((first_ref, FIRST, 16), (second_ref, SECOND, 8)):
            gap = 8 if slots == 16 else 3
            for part in range(2):
                for jj, j in enumerate(tiles):
                    v = t_ref[pl.ds(d * 36 + half + j * 2 + part, 3, stride=6), :]
                    ref[pl.ds(d * slots + part * gap + jj * 3, 3), :] = v
        return 0

    lax.fori_loop(0, NDISP, one, 0, unroll=4)


def translate_kernel(tiles, src_ref, disp_ref, own_ref, other_ref, t_ref, out_ref, s_ref):
    n, half, box, rows = shape_of(tiles)
    step = 8 if n == 1 else 16

    def lay(i, _):
        for first, ref in ((0, own_ref), (CHIPS, other_ref)):
            for p in range(PARENTS):
                re = ref[pl.ds(i * rows + p * box, half), :]
                im = ref[pl.ds(i * rows + p * box + half, half), :]
                to = ((first + i) * PARENTS + p) * 16
                s_ref[pl.ds(to, half), :] = re
                s_ref[pl.ds(to + 8, half), :] = im
                if n == 1:
                    s_ref[pl.ds(to + 3, half), :] = im
                    s_ref[pl.ds(to + 11, half), :] = re
        return 0

    lax.fori_loop(0, CHIPS, lay, 0, unroll=2)

    def receiver(i, _):
        sums = None
        for q in range(NPART):
            at = i * NPART + q
            a = pl.multiple_of(src_ref[at] * 16, 8)
            d = pl.multiple_of(disp_ref[at] * step, 8)
            s0, s1 = s_ref[pl.ds(a, 8), :], s_ref[pl.ds(a + 8, 8), :]
            t0 = t_ref[pl.ds(d, 8), :]
            if n == 1:
                terms = (t0 * s0, t0 * s1)
            else:
                t1 = t_ref[pl.ds(d + 8, 8), :]
                terms = (t0 * s0, t1 * s1, t0 * s1, t1 * s0)
            sums = terms if q == 0 else tuple(x + y for x, y in zip(sums, terms))
        if n == 1:
            re, im = sums[0][0:3] - sums[0][3:6], sums[1][0:3] + sums[1][3:6]
        else:
            re, im = (sums[0] - sums[1])[:half], (sums[2] + sums[3])[:half]
        to = (i // PARENTS) * rows + (i % PARENTS) * box
        out_ref[pl.ds(to, half), :] = re
        out_ref[pl.ds(to + half, half), :] = im
        return 0

    lax.fori_loop(0, CHIPS * PARENTS, receiver, 0, unroll=2)


def disaggregate_kernel(tiles, oct_ref, x_ref, cos_ref, sin_ref, ti_ref, tw_ref, pi_ref, pw_ref, *rest):
    (*before_ref, out_ref, t_ref, pe_ref, po_ref, in_ref, r3_ref, z3_ref) = rest
    n, half, box, rows = shape_of(tiles)
    p = pl.program_id(0)
    columns = slice(tiles[0] * 128, tiles[0] * 128 + n * 128)

    @pl.when(p == 0)
    def _():
        hi, lo = split(stencil_t(ti_ref[...], tw_ref[...], NT1, even_odd))
        t_ref[...] = jnp.concatenate([hi, hi, lo], axis=1)
        for ref, shift in ((pe_ref, 0), (po_ref, 64)):
            m = jnp.transpose(stencil_t(pi_ref[:, columns], pw_ref[:, columns], 256, lambda a: a + shift))
            hi, lo = split(m)
            ref[...] = jnp.concatenate([hi, hi, lo], axis=0)

    for part in range(2):
        for j in range(n):
            for r in range(3):
                base = p * box + part * half + j * 3 + r
                for zh in range(2):
                    v = x_ref[pl.ds(zh * 32 * rows + base, 32, stride=rows), :]
                    in_ref[2 * j + part, pl.ds(3 * zh + r, 32, stride=6), :] = v

    for k in range(8):
        o = oct_ref[p, k]
        for j in range(n):
            re, im = in_ref[2 * j], in_ref[2 * j + 1]
            c = cos_ref[o, :, j * 128 : j * 128 + 128]
            s = sin_ref[o, :, j * 128 : j * 128 + 128]
            slot = (k * n + j) % 4
            for part, v in ((0, re * c + im * s), (1, im * c - re * s)):
                hi, lo = split(v)
                cols = slice(part * 128, part * 128 + 128)
                r3_ref[slot, 0:192, cols] = hi
                r3_ref[slot, 192:384, cols] = lo
                r3_ref[slot, 384:576, cols] = hi
            z = dot(t_ref[...], r3_ref[slot])
            hi, lo = split(z)
            for part in range(2):
                for odd in range(2):
                    for base, v in ((0, hi), (n * 128, lo), (n * 256, hi)):
                        row = (k * 2 + part) * 48
                        z3_ref[odd, row : row + 48, base + j * 128 : base + j * 128 + 128] = v[
                            odd * 48 : odd * 48 + 48, part * 128 : part * 128 + 128
                        ]

    for k in range(8):
        span = slice(k * 96, k * 96 + 96)
        even = dot(z3_ref[0, span, :], pe_ref[...])
        odd = dot(z3_ref[1, span, :], po_ref[...])
        blocks = (even[:, :128], even[:, 128:] + odd[:, :128], odd[:, 128:])
        for part in range(2):
            for tile in range(3):
                to = pl.ds(k * 288 + 2 * tile + part, 48, stride=6)
                v = blocks[tile][part * 48 : part * 48 + 48]
                out_ref[to, :] = v + before_ref[0][to, :] if before_ref else v


def whole(shape):
    return pl.BlockSpec(shape, lambda *_: (0,) * len(shape))


VMEM = pl.BlockSpec(memory_space=pltpu.VMEM)
SMEM = pl.BlockSpec(memory_space=pltpu.SMEM)
STENCILS = [whole((4, NT2)), whole((4, NT2)), whole((4, NP2)), whole((4, NP2))]
PARAMS = pltpu.CompilerParams(vmem_limit_bytes=60 * 2**20)
CHILDREN = pl.BlockSpec((8 * 288, 128), lambda p: (p, 0))


def cost(flops, nbytes):
    return pl.CostEstimate(flops=flops, bytes_accessed=nbytes, transcendentals=0)


def table_of(tiles):
    n = len(tiles)
    return pl.BlockSpec((8, NT2, 128 * n), lambda p: (0, 0, tiles[0] // n))


def aggregate(tiles, tables):
    n, _, _, rows = shape_of(tiles)
    table = (8, NT2, NP2)
    part = (8, NT2, 128 * n)
    shapes = [jax.ShapeDtypeStruct((CHIPS * rows, 128), F32)]
    specs = [whole((CHIPS * rows, 128))]
    trig = []
    if tables:
        shapes += [jax.ShapeDtypeStruct(table, F32)] * 2
        specs += [whole(table)] * 2
    else:
        trig = [pltpu.VMEM(part, F32)] * 2
    return pl.pallas_call(
        functools.partial(aggregate_kernel, tiles, tables),
        grid=(PARENTS,),
        in_specs=[SMEM, CHILDREN, whole(table) if tables else table_of(tiles), *STENCILS],
        out_specs=specs,
        out_shape=shapes,
        scratch_shapes=trig
        + [
            pltpu.VMEM((NT2, 288), BF16),
            pltpu.VMEM((2, 256, 128 * n), BF16),
            pltpu.VMEM((2, 256, 128 * n), BF16),
            pltpu.VMEM((768, 384), BF16),
            pltpu.VMEM((768, 384), BF16),
            pltpu.VMEM((8, 288, 256 * n), BF16),
            pltpu.VMEM((2 * n, NT2, 128), F32),
        ],
        compiler_params=PARAMS,
        cost_estimate=cost(n * 4 * 10**9, 10**7),
        name=f"aggregate{n}",
    )


def operators():
    return pl.pallas_call(
        operators_kernel,
        in_specs=[SMEM, VMEM],
        out_specs=[VMEM, VMEM],
        out_shape=[jax.ShapeDtypeStruct((NDISP * 16, 128), F32), jax.ShapeDtypeStruct((NDISP * 8, 128), F32)],
        compiler_params=PARAMS,
        cost_estimate=cost(10**6, 10**7),
        name="operators",
    )


def translate(tiles):
    n, _, _, rows = shape_of(tiles)
    return pl.pallas_call(
        functools.partial(translate_kernel, tiles),
        in_specs=[SMEM, SMEM, VMEM, VMEM, VMEM],
        out_specs=VMEM,
        out_shape=jax.ShapeDtypeStruct((CHIPS * rows, 128), F32),
        scratch_shapes=[pltpu.VMEM((512 * 16, 128), F32)],
        compiler_params=PARAMS,
        cost_estimate=cost(10**8, 10**7),
        name=f"translate{n}",
    )


def disaggregate(tiles, more):
    n, _, _, rows = shape_of(tiles)
    return pl.pallas_call(
        functools.partial(disaggregate_kernel, tiles),
        grid=(PARENTS,),
        in_specs=[SMEM, whole((CHIPS * rows, 128)), table_of(tiles), table_of(tiles), *STENCILS] + [CHILDREN] * more,
        out_specs=CHILDREN,
        out_shape=jax.ShapeDtypeStruct((32 * 288, 128), F32),
        scratch_shapes=[
            pltpu.VMEM((NT1, 576), BF16),
            pltpu.VMEM((384 * n, 256), BF16),
            pltpu.VMEM((384 * n, 256), BF16),
            pltpu.VMEM((2 * n, NT2, 128), F32),
            pltpu.VMEM((4, 576, 256), BF16),
            pltpu.VMEM((2, 768, 384 * n), BF16),
        ],
        compiler_params=PARAMS,
        cost_estimate=cost(n * 4 * 10**9, 10**7),
        name=f"disaggregate{n}",
    )


def exchange(a):
    return lax.all_to_all(a.reshape(CHIPS, -1, 128), CHIP, 0, 0, tiled=True).reshape(a.shape)


def together(*arrays):
    return lax.optimization_barrier(arrays)


def local(
    child_out, child_octant, theta_index, theta_weight, phi_index, phi_weight,
    shift_angle, partner_src, partner_disp, translation,
):
    core = lax.axis_index("c")
    zh = lax.axis_index("zh")
    swap = [(0, 1), (1, 0)]
    x = child_out.reshape(32, 2, 144, 128).transpose(0, 2, 1, 3).reshape(32 * 288, 128)
    stencils = (theta_index.T, theta_weight.T, phi_index.T, phi_weight.T)

    def mine(a):
        return lax.dynamic_index_in_dim(a.reshape(2, 2, 128, NPART), core, 1, keepdims=False).reshape(-1)

    src = mine(partner_src)
    holder, p = src // 4, src % 4
    far = jnp.where((holder // 32) % 2 == core, 0, 1)
    src_at = (far * CHIPS + (holder // 64) * 32 + holder % 32) * PARENTS + p
    disp_at = mine(partner_disp)
    ops, = together(translation.transpose(0, 2, 1, 3).reshape(NDISP * 6, 2, NP2))
    ops = ops.reshape(NDISP * 6, 2, 3, 128).transpose(0, 2, 1, 3).reshape(NDISP * 36, 128)

    (out1,) = aggregate(FIRST, False)(child_octant, x, shift_angle, *stencils)
    got1 = exchange(out1)
    x2, _ = together(x, out1)
    out2, cosine, sine = aggregate(SECOND, True)(child_octant, x2, shift_angle, *stencils)
    ops1, ops2 = operators()(zh.reshape(1), ops)
    got1, out2, ops1, ops2, src_at, disp_at = together(got1, out2, ops1, ops2, src_at, disp_at)

    got2 = exchange(out2)
    other1 = lax.ppermute(got1, "c", swap)
    in1 = translate(FIRST)(src_at, disp_at, got1, other1, ops1)
    in1, got2 = together(in1, got2)

    back1 = exchange(in1)
    other2 = lax.ppermute(got2, "c", swap)
    in2 = translate(SECOND)(src_at, disp_at, got2, other2, ops2)
    in2, back1 = together(in2, back1)

    back2 = exchange(in2)
    y = disaggregate(FIRST, 0)(child_octant, back1, cosine, sine, *stencils)
    y, back2 = together(y, back2)
    y = disaggregate(SECOND, 1)(child_octant, back2, cosine, sine, *stencils, y)
    return y.reshape(32, 144, 2, 128).transpose(0, 2, 1, 3).reshape(32, 2, NT1 * NP1)


def solution(mesh):
    fine = Mesh(mesh.devices.reshape(2, 2, 2, 4, 4), ALL)
    boxes = P(ALL)
    in_specs = (boxes, boxes, P(), P(), P(), P(), P(), P(), P(), P(None, None, ("zl", "y", "x"), None))
    return jax.shard_map(local, mesh=fine, in_specs=in_specs, out_specs=boxes, check_vma=False)
```

```python
import functools

import jax
import jax.numpy as jnp
import numpy as np
from jax import lax
from jax.experimental import pallas as pl
from jax.experimental.pallas import tpu as pltpu
from jax.sharding import Mesh, PartitionSpec as P

NT1, NP1, NT2, NP2 = 96, 192, 192, 384
NDISP, NPART = 316, 32
CHIPS = 64
PARENTS = 4
SLOT = 16
FIRST, SECOND = (0, 1), (2,)
F32, BF16 = jnp.float32, jnp.bfloat16
ALL = ("zh", "c", "zl", "y", "x")
CHIP = ("zh", "zl", "y", "x")


def fit(fn, powers):
    h = 0.7855 * (1 - np.cos(np.pi * (np.arange(400) + 0.5) / 400))
    a = np.stack([h**k for k in powers], 1)
    return [float(v) for v in np.linalg.lstsq(a, fn(h), rcond=None)[0]]


SIN = fit(np.sin, (1, 3, 5, 7, 9, 11))
COS = fit(np.cos, (0, 2, 4, 6, 8, 10))


def horner(z, coefs):
    r = jnp.full_like(z, coefs[-1])
    for c in coefs[-2::-1]:
        r = r * z + c
    return r


def split(x):
    hi = x.astype(BF16)
    return hi, (x - hi.astype(F32)).astype(BF16)


def dot(a, b):
    return jnp.dot(a, b, preferred_element_type=F32)


def stencil_t(index, weight, rows, target):
    n = index.shape[1]
    row = lax.broadcasted_iota(jnp.int32, (rows, n), 0)
    out = jnp.zeros((rows, n), F32)
    for j in range(4):
        out = out + jnp.where(row == target(index[j : j + 1, :]), weight[j : j + 1, :], 0.0)
    return out


def even_odd(a):
    return jnp.where(a % 2 == 0, a // 2, 48 + a // 2)


def shape_of(tiles):
    n = len(tiles)
    return n, 3 * n, 6 * n, 24 * n


def aggregate_kernel(tiles, tables, oct_ref, x_ref, angle_ref, ti_ref, tw_ref, pi_ref, pw_ref, out_ref, cos_ref, sin_ref, *scratch):
    t3_ref, pe_ref, po_ref, vh_ref, vl_ref, y3_ref, acc_ref = scratch
    n, half, box, rows = shape_of(tiles)
    p = pl.program_id(0)
    first = tiles[0] if tables else 0
    columns = slice(tiles[0] * 128, tiles[0] * 128 + n * 128)

    @pl.when(p == 0)
    def _():
        def trig(o, _):
            for r in range(0, NT2, 48):
                h = angle_ref[o, r : r + 48, :] * 0.5
                z = h * h
                s = horner(z, SIN) * h
                c = horner(z, COS)
                cos_ref[o, r : r + 48, :] = 1.0 - 2.0 * (s * s)
                sin_ref[o, r : r + 48, :] = 2.0 * (s * c)
            return 0

        lax.fori_loop(0, 8, trig, 0)
        tt = stencil_t(ti_ref[...], tw_ref[...], 128, even_odd)
        t = jnp.transpose(jnp.concatenate([tt, jnp.zeros((128, 64), F32)], axis=1))[:NT2, :NT1]
        hi, lo = split(t)
        t3_ref[...] = jnp.concatenate([hi, hi, lo], axis=1)
        for ref, shift in ((pe_ref, 0), (po_ref, 64)):
            hi, lo = split(stencil_t(pi_ref[:, columns], pw_ref[:, columns], 256, lambda a: a + shift))
            ref[0], ref[1] = hi, lo

    for k in range(8):
        for part in range(2):
            row = (k * 2 + part) * 48
            for tile in range(3):
                v = x_ref[pl.ds(k * 288 + 2 * tile + part, 48, stride=6), :]
                hi, lo = split(v)
                vh_ref[row : row + 48, tile * 128 : tile * 128 + 128] = hi
                vl_ref[row : row + 48, tile * 128 : tile * 128 + 128] = lo
    for odd, ref in ((0, pe_ref), (1, po_ref)):
        cols = slice(odd * 128, odd * 128 + 256)
        for m in range(0, 768, 192):
            vh, vl = vh_ref[m : m + 192, cols], vl_ref[m : m + 192, cols]
            y = dot(vh, ref[0]) + dot(vl, ref[0]) + dot(vh, ref[1])
            yh, yl = split(y)
            for kk in range(2):
                for part in range(2):
                    r = (kk * 2 + part) * 48
                    for j in range(n):
                        col = j * 256 + part * 128
                        for base, v in ((0, yh), (96, yl), (192, yh)):
                            y3_ref[m // 96 + kk, base + odd * 48 : base + odd * 48 + 48, col : col + 128] = v[
                                r : r + 48, j * 128 : j * 128 + 128
                            ]

    for k in range(8):
        o = oct_ref[p, k]
        for j in range(n):
            f = dot(t3_ref[...], y3_ref[k, :, j * 256 : j * 256 + 256])
            re, im = f[:, :128], f[:, 128:]
            at = (first + j) * 128
            c = cos_ref[o, :, at : at + 128]
            s = sin_ref[o, :, at : at + 128]
            if k == 0:
                acc_ref[2 * j] = re * c - im * s
                acc_ref[2 * j + 1] = re * s + im * c
            else:
                acc_ref[2 * j] += re * c - im * s
                acc_ref[2 * j + 1] += re * s + im * c

    for part in range(2):
        for j in range(n):
            for r in range(3):
                base = p * box + part * half + j * 3 + r
                for zh in range(2):
                    v = acc_ref[2 * j + part, pl.ds(3 * zh + r, 32, stride=6), :]
                    out_ref[pl.ds(zh * 32 * rows + base, 32, stride=rows), :] = v


def operators_kernel(zh_ref, t_ref, first_ref, second_ref):
    half = zh_ref[0] * 18

    def one(d, _):
        for ref, tiles in ((first_ref, FIRST), (second_ref, SECOND)):
            gap = 8 if len(tiles) == 2 else 3
            for part in range(2):
                for jj, j in enumerate(tiles):
                    v = t_ref[pl.ds(d * 36 + half + j * 2 + part, 3, stride=6), :]
                    ref[pl.ds(d * SLOT + part * gap + jj * 3, 3), :] = v
        return 0

    lax.fori_loop(0, NDISP, one, 0, unroll=4)


def translate_kernel(tiles, src_ref, disp_ref, own_ref, other_ref, t_ref, out_ref, s_ref):
    n, half, box, rows = shape_of(tiles)

    def lay(i, _):
        for first, ref in ((0, own_ref), (CHIPS, other_ref)):
            for p in range(PARENTS):
                re = ref[pl.ds(i * rows + p * box, half), :]
                im = ref[pl.ds(i * rows + p * box + half, half), :]
                to = ((first + i) * PARENTS + p) * 16
                s_ref[pl.ds(to, half), :] = re
                s_ref[pl.ds(to + 8, half), :] = im
                if n == 1:
                    s_ref[pl.ds(to + 3, half), :] = im
                    s_ref[pl.ds(to + 11, half), :] = re
        return 0

    lax.fori_loop(0, CHIPS, lay, 0, unroll=2)

    def receiver(i, _):
        sums = None
        for q in range(NPART):
            at = i * NPART + q
            a = pl.multiple_of(src_ref[at], 8)
            d = pl.multiple_of(disp_ref[at], 8)
            s0, s1 = s_ref[pl.ds(a, 8), :], s_ref[pl.ds(a + 8, 8), :]
            t0 = t_ref[pl.ds(d, 8), :]
            if n == 1:
                terms = (t0 * s0, t0 * s1)
            else:
                t1 = t_ref[pl.ds(d + 8, 8), :]
                terms = (t0 * s0, t1 * s1, t0 * s1, t1 * s0)
            sums = terms if q == 0 else tuple(x + y for x, y in zip(sums, terms))
        if n == 1:
            re, im = sums[0][0:3] - sums[0][3:6], sums[1][0:3] + sums[1][3:6]
        else:
            re, im = (sums[0] - sums[1])[:half], (sums[2] + sums[3])[:half]
        to = (i // PARENTS) * rows + (i % PARENTS) * box
        out_ref[pl.ds(to, half), :] = re
        out_ref[pl.ds(to + half, half), :] = im
        return 0

    lax.fori_loop(0, CHIPS * PARENTS, receiver, 0, unroll=2)


def disaggregate_kernel(tiles, oct_ref, x_ref, cos_ref, sin_ref, ti_ref, tw_ref, pi_ref, pw_ref, *rest):
    (*before_ref, out_ref, t_ref, pe_ref, po_ref, in_ref, z3_ref) = rest
    n, half, box, rows = shape_of(tiles)
    p = pl.program_id(0)
    columns = slice(tiles[0] * 128, tiles[0] * 128 + n * 128)

    @pl.when(p == 0)
    def _():
        t_ref[...] = jnp.concatenate(split(stencil_t(ti_ref[...], tw_ref[...], NT1, even_odd)), axis=0)
        for ref, shift in ((pe_ref, 0), (po_ref, 64)):
            m = jnp.transpose(stencil_t(pi_ref[:, columns], pw_ref[:, columns], 256, lambda a: a + shift))
            hi, lo = split(m)
            ref[...] = jnp.concatenate([hi, hi, lo], axis=0)

    for part in range(2):
        for j in range(n):
            for r in range(3):
                base = p * box + part * half + j * 3 + r
                for zh in range(2):
                    v = x_ref[pl.ds(zh * 32 * rows + base, 32, stride=rows), :]
                    in_ref[2 * j + part, pl.ds(3 * zh + r, 32, stride=6), :] = v

    for k in range(8):
        o = oct_ref[p, k]
        for j in range(n):
            re, im = in_ref[2 * j], in_ref[2 * j + 1]
            c = cos_ref[o, :, j * 128 : j * 128 + 128]
            s = sin_ref[o, :, j * 128 : j * 128 + 128]
            hi, lo = split(jnp.concatenate([re * c + im * s, im * c - re * s], axis=1))
            g = dot(t_ref[...], hi)
            z = g[:NT1] + g[NT1:] + dot(t_ref[:NT1], lo)
            hi, lo = split(z)
            for part in range(2):
                for odd in range(2):
                    for base, v in ((0, hi), (n * 128, lo), (n * 256, hi)):
                        row = (k * 2 + part) * 48
                        z3_ref[odd, row : row + 48, base + j * 128 : base + j * 128 + 128] = v[
                            odd * 48 : odd * 48 + 48, part * 128 : part * 128 + 128
                        ]

    for first in range(0, 8, 4):
        span = slice(first * 96, first * 96 + 384)
        even = dot(z3_ref[0, span, :], pe_ref[...])
        odd = dot(z3_ref[1, span, :], po_ref[...])
        blocks = (even[:, :128], even[:, 128:] + odd[:, :128], odd[:, 128:])
        for k in range(4):
            for part in range(2):
                at = (k * 2 + part) * 48
                for tile in range(3):
                    to = pl.ds((first + k) * 288 + 2 * tile + part, 48, stride=6)
                    v = blocks[tile][at : at + 48]
                    out_ref[to, :] = v + before_ref[0][to, :] if before_ref else v


def whole(shape):
    return pl.BlockSpec(shape, lambda *_: (0,) * len(shape))


VMEM = pl.BlockSpec(memory_space=pltpu.VMEM)
SMEM = pl.BlockSpec(memory_space=pltpu.SMEM)
STENCILS = [whole((4, NT2)), whole((4, NT2)), whole((4, NP2)), whole((4, NP2))]
PARAMS = pltpu.CompilerParams(vmem_limit_bytes=60 * 2**20)
CHILDREN = pl.BlockSpec((8 * 288, 128), lambda p: (p, 0))


def cost(flops, nbytes):
    return pl.CostEstimate(flops=flops, bytes_accessed=nbytes, transcendentals=0)


def table_of(tiles):
    n = len(tiles)
    return pl.BlockSpec((8, NT2, 128 * n), lambda p: (0, 0, tiles[0] // n))


def aggregate(tiles, tables):
    n, _, _, rows = shape_of(tiles)
    table = (8, NT2, NP2)
    part = (8, NT2, 128 * n)
    shapes = [jax.ShapeDtypeStruct((CHIPS * rows, 128), F32)]
    specs = [whole((CHIPS * rows, 128))]
    trig = []
    if tables:
        shapes += [jax.ShapeDtypeStruct(table, F32)] * 2
        specs += [whole(table)] * 2
    else:
        trig = [pltpu.VMEM(part, F32)] * 2
    return pl.pallas_call(
        functools.partial(aggregate_kernel, tiles, tables),
        grid=(PARENTS,),
        in_specs=[SMEM, CHILDREN, whole(table) if tables else table_of(tiles), *STENCILS],
        out_specs=specs,
        out_shape=shapes,
        scratch_shapes=trig
        + [
            pltpu.VMEM((NT2, 288), BF16),
            pltpu.VMEM((2, 256, 128 * n), BF16),
            pltpu.VMEM((2, 256, 128 * n), BF16),
            pltpu.VMEM((768, 384), BF16),
            pltpu.VMEM((768, 384), BF16),
            pltpu.VMEM((8, 288, 256 * n), BF16),
            pltpu.VMEM((2 * n, NT2, 128), F32),
        ],
        compiler_params=PARAMS,
        cost_estimate=cost(n * 4 * 10**9, 10**7),
        name=f"aggregate{n}",
    )


def operators():
    return pl.pallas_call(
        operators_kernel,
        in_specs=[SMEM, VMEM],
        out_specs=[VMEM, VMEM],
        out_shape=[jax.ShapeDtypeStruct((NDISP * SLOT, 128), F32)] * 2,
        compiler_params=PARAMS,
        cost_estimate=cost(10**6, 10**7),
        name="operators",
    )


def translate(tiles):
    n, _, _, rows = shape_of(tiles)
    return pl.pallas_call(
        functools.partial(translate_kernel, tiles),
        in_specs=[SMEM, SMEM, VMEM, VMEM, VMEM],
        out_specs=VMEM,
        out_shape=jax.ShapeDtypeStruct((CHIPS * rows, 128), F32),
        scratch_shapes=[pltpu.VMEM((512 * 16, 128), F32)],
        compiler_params=PARAMS,
        cost_estimate=cost(10**8, 10**7),
        name=f"translate{n}",
    )


def disaggregate(tiles, more):
    n, _, _, rows = shape_of(tiles)
    return pl.pallas_call(
        functools.partial(disaggregate_kernel, tiles),
        grid=(PARENTS,),
        in_specs=[SMEM, whole((CHIPS * rows, 128)), table_of(tiles), table_of(tiles), *STENCILS] + [CHILDREN] * more,
        out_specs=CHILDREN,
        out_shape=jax.ShapeDtypeStruct((32 * 288, 128), F32),
        scratch_shapes=[
            pltpu.VMEM((2 * NT1, NT2), BF16),
            pltpu.VMEM((384 * n, 256), BF16),
            pltpu.VMEM((384 * n, 256), BF16),
            pltpu.VMEM((2 * n, NT2, 128), F32),
            pltpu.VMEM((2, 768, 384 * n), BF16),
        ],
        compiler_params=PARAMS,
        cost_estimate=cost(n * 4 * 10**9, 10**7),
        name=f"disaggregate{n}",
    )


def exchange(a):
    return lax.all_to_all(a.reshape(CHIPS, -1, 128), CHIP, 0, 0, tiled=True).reshape(a.shape)


def together(*arrays):
    return lax.optimization_barrier(arrays)


def local(
    child_out, child_octant, theta_index, theta_weight, phi_index, phi_weight,
    shift_angle, partner_src, partner_disp, translation,
):
    core = lax.axis_index("c")
    zh = lax.axis_index("zh")
    swap = [(0, 1), (1, 0)]
    x = child_out.reshape(32, 2, 144, 128).transpose(0, 2, 1, 3).reshape(32 * 288, 128)
    stencils = (theta_index.T, theta_weight.T, phi_index.T, phi_weight.T)

    def mine(a):
        return lax.dynamic_index_in_dim(a.reshape(2, 2, 128, NPART), core, 1, keepdims=False).reshape(-1)

    src = mine(partner_src)
    holder, p = src // 4, src % 4
    far = jnp.where((holder // 32) % 2 == core, 0, 1)
    src_at = ((far * CHIPS + (holder // 64) * 32 + holder % 32) * PARENTS + p) * SLOT
    disp_at = mine(partner_disp) * SLOT
    ops, = together(translation.transpose(0, 2, 1, 3).reshape(NDISP * 6, 2, NP2))
    ops = ops.reshape(NDISP * 6, 2, 3, 128).transpose(0, 2, 1, 3).reshape(NDISP * 36, 128)

    (out1,) = aggregate(FIRST, False)(child_octant, x, shift_angle, *stencils)
    got1 = exchange(out1)
    x2, _ = together(x, out1)
    out2, cosine, sine = aggregate(SECOND, True)(child_octant, x2, shift_angle, *stencils)
    ops1, ops2 = operators()(zh.reshape(1), ops)
    got1, out2, ops1, ops2, src_at, disp_at = together(got1, out2, ops1, ops2, src_at, disp_at)

    got2 = exchange(out2)
    other1 = lax.ppermute(got1, "c", swap)
    in1 = translate(FIRST)(src_at, disp_at, got1, other1, ops1)
    in1, got2 = together(in1, got2)

    back1 = exchange(in1)
    other2 = lax.ppermute(got2, "c", swap)
    in2 = translate(SECOND)(src_at, disp_at, got2, other2, ops2)
    in2, back1 = together(in2, back1)

    back2 = exchange(in2)
    y = disaggregate(FIRST, 0)(child_octant, back1, cosine, sine, *stencils)
    y, back2 = together(y, back2)
    y = disaggregate(SECOND, 1)(child_octant, back2, cosine, sine, *stencils, y)
    return y.reshape(32, 144, 2, 128).transpose(0, 2, 1, 3).reshape(32, 2, NT1 * NP1)


def solution(mesh):
    fine = Mesh(mesh.devices.reshape(2, 2, 2, 4, 4), ALL)
    boxes = P(ALL)
    in_specs = (boxes, boxes, P(), P(), P(), P(), P(), P(), P(), P(None, None, ("zl", "y", "x"), None))
    return jax.shard_map(local, mesh=fine, in_specs=in_specs, out_specs=boxes, check_vma=False)
```

```python
import functools

import jax
import jax.numpy as jnp
import numpy as np
from jax import lax
from jax.experimental import pallas as pl
from jax.experimental.pallas import tpu as pltpu
from jax.sharding import Mesh, PartitionSpec as P

NT1, NP1, NT2, NP2 = 96, 192, 192, 384
NDISP, NPART = 316, 32
CHIPS = 64
PARENTS = 4
BOXES = CHIPS * PARENTS
SLOT = 16
FIRST, SECOND = (0, 1), (2,)
F32, BF16 = jnp.float32, jnp.bfloat16
ALL = ("zh", "c", "zl", "y", "x")
CHIP = ("zh", "zl", "y", "x")


def fit(fn, powers):
    h = 0.7855 * (1 - np.cos(np.pi * (np.arange(400) + 0.5) / 400))
    a = np.stack([h**k for k in powers], 1)
    return [float(v) for v in np.linalg.lstsq(a, fn(h), rcond=None)[0]]


SIN = fit(np.sin, (1, 3, 5, 7, 9, 11))
COS = fit(np.cos, (0, 2, 4, 6, 8, 10))


def horner(z, coefs):
    r = jnp.full_like(z, coefs[-1])
    for c in coefs[-2::-1]:
        r = r * z + c
    return r


def split(x):
    hi = x.astype(BF16)
    return hi, (x - hi.astype(F32)).astype(BF16)


def dot(a, b):
    return jnp.dot(a, b, preferred_element_type=F32)


def stencil_t(index, weight, rows, target):
    n = index.shape[1]
    row = lax.broadcasted_iota(jnp.int32, (rows, n), 0)
    out = jnp.zeros((rows, n), F32)
    for j in range(4):
        out = out + jnp.where(row == target(index[j : j + 1, :]), weight[j : j + 1, :], 0.0)
    return out


def even_odd(a):
    return jnp.where(a % 2 == 0, a // 2, 48 + a // 2)


def shape_of(tiles):
    n = len(tiles)
    return n, 3 * n, 6 * n, 24 * n


def aggregate_kernel(tiles, tables, oct_ref, x_ref, angle_ref, ti_ref, tw_ref, pi_ref, pw_ref, out_ref, cos_ref, sin_ref, *scratch):
    t3_ref, pe_ref, po_ref, vh_ref, vl_ref, y3_ref, acc_ref = scratch
    n, half, box, rows = shape_of(tiles)
    p = pl.program_id(0)
    first = tiles[0] if tables else 0
    columns = slice(tiles[0] * 128, tiles[0] * 128 + n * 128)

    @pl.when(p == 0)
    def _():
        def trig(o, _):
            for r in range(0, NT2, 48):
                h = angle_ref[o, r : r + 48, :] * 0.5
                z = h * h
                s = horner(z, SIN) * h
                c = horner(z, COS)
                cos_ref[o, r : r + 48, :] = 1.0 - 2.0 * (s * s)
                sin_ref[o, r : r + 48, :] = 2.0 * (s * c)
            return 0

        lax.fori_loop(0, 8, trig, 0)
        tt = stencil_t(ti_ref[...], tw_ref[...], 128, even_odd)
        t = jnp.transpose(jnp.concatenate([tt, jnp.zeros((128, 64), F32)], axis=1))[:NT2, :NT1]
        hi, lo = split(t)
        t3_ref[...] = jnp.concatenate([hi, hi, lo], axis=1)
        for ref, shift in ((pe_ref, 0), (po_ref, 64)):
            hi, lo = split(stencil_t(pi_ref[:, columns], pw_ref[:, columns], 256, lambda a: a + shift))
            ref[0], ref[1] = hi, lo

    for k in range(8):
        for part in range(2):
            row = (k * 2 + part) * 48
            for tile in range(3):
                v = x_ref[pl.ds(k * 288 + 2 * tile + part, 48, stride=6), :]
                hi, lo = split(v)
                vh_ref[row : row + 48, tile * 128 : tile * 128 + 128] = hi
                vl_ref[row : row + 48, tile * 128 : tile * 128 + 128] = lo
    for odd, ref in ((0, pe_ref), (1, po_ref)):
        cols = slice(odd * 128, odd * 128 + 256)
        for m in range(0, 768, 192):
            vh, vl = vh_ref[m : m + 192, cols], vl_ref[m : m + 192, cols]
            y = dot(vh, ref[0]) + dot(vl, ref[0]) + dot(vh, ref[1])
            yh, yl = split(y)
            for kk in range(2):
                for part in range(2):
                    r = (kk * 2 + part) * 48
                    for j in range(n):
                        col = j * 256 + part * 128
                        for base, v in ((0, yh), (96, yl), (192, yh)):
                            y3_ref[m // 96 + kk, base + odd * 48 : base + odd * 48 + 48, col : col + 128] = v[
                                r : r + 48, j * 128 : j * 128 + 128
                            ]

    for k in range(8):
        o = oct_ref[p, k]
        for j in range(n):
            f = dot(t3_ref[...], y3_ref[k, :, j * 256 : j * 256 + 256])
            re, im = f[:, :128], f[:, 128:]
            at = (first + j) * 128
            c = cos_ref[o, :, at : at + 128]
            s = sin_ref[o, :, at : at + 128]
            if k == 0:
                acc_ref[2 * j] = re * c - im * s
                acc_ref[2 * j + 1] = re * s + im * c
            else:
                acc_ref[2 * j] += re * c - im * s
                acc_ref[2 * j + 1] += re * s + im * c

    for part in range(2):
        for j in range(n):
            for r in range(3):
                base = p * box + part * half + j * 3 + r
                for zh in range(2):
                    v = acc_ref[2 * j + part, pl.ds(3 * zh + r, 32, stride=6), :]
                    out_ref[pl.ds(zh * 32 * rows + base, 32, stride=rows), :] = v


def operators_kernel(zh_ref, t_ref, first_ref, second_ref):
    half = zh_ref[0] * 18

    def one(d, _):
        for ref, tiles in ((first_ref, FIRST), (second_ref, SECOND)):
            gap = 8 if len(tiles) == 2 else 3
            for part in range(2):
                for jj, j in enumerate(tiles):
                    v = t_ref[pl.ds(d * 36 + half + j * 2 + part, 3, stride=6), :]
                    ref[pl.ds(d * SLOT + part * gap + jj * 3, 3), :] = v
        return 0

    lax.fori_loop(0, NDISP, one, 0, unroll=4)


def translate_kernel(tiles, src_ref, disp_ref, own_ref, other_ref, t_ref, out_ref, s_ref):
    n, half, box, rows = shape_of(tiles)

    def lay(i, _):
        for first, ref in ((0, own_ref), (CHIPS, other_ref)):
            for p in range(PARENTS):
                re = ref[pl.ds(i * rows + p * box, half), :]
                im = ref[pl.ds(i * rows + p * box + half, half), :]
                to = ((first + i) * PARENTS + p) * 16
                s_ref[pl.ds(to, half), :] = re
                s_ref[pl.ds(to + 8, half), :] = im
                if n == 1:
                    s_ref[pl.ds(to + 3, half), :] = im
                    s_ref[pl.ds(to + 11, half), :] = re
        return 0

    lax.fori_loop(0, CHIPS, lay, 0, unroll=2)

    def receiver(i, _):
        sums = None
        for q in range(NPART):
            a = pl.multiple_of(src_ref.at[pl.ds(q * BOXES, BOXES)][i], 8)
            d = pl.multiple_of(disp_ref.at[pl.ds(q * BOXES, BOXES)][i], 8)
            s0, s1 = s_ref[pl.ds(a, 8), :], s_ref[pl.ds(a + 8, 8), :]
            t0 = t_ref[pl.ds(d, 8), :]
            if n == 1:
                terms = (t0 * s0, t0 * s1)
            else:
                t1 = t_ref[pl.ds(d + 8, 8), :]
                terms = (t0 * s0, t1 * s1, t0 * s1, t1 * s0)
            sums = terms if q == 0 else tuple(x + y for x, y in zip(sums, terms))
        if n == 1:
            re, im = sums[0][0:3] - sums[0][3:6], sums[1][0:3] + sums[1][3:6]
        else:
            re, im = (sums[0] - sums[1])[:half], (sums[2] + sums[3])[:half]
        to = (i // PARENTS) * rows + (i % PARENTS) * box
        out_ref[pl.ds(to, half), :] = re
        out_ref[pl.ds(to + half, half), :] = im
        return 0

    lax.fori_loop(0, CHIPS * PARENTS, receiver, 0, unroll=2)


def disaggregate_kernel(tiles, oct_ref, x_ref, cos_ref, sin_ref, ti_ref, tw_ref, pi_ref, pw_ref, *rest):
    (*before_ref, out_ref, t_ref, pe_ref, po_ref, in_ref, z3_ref) = rest
    n, half, box, rows = shape_of(tiles)
    p = pl.program_id(0)
    columns = slice(tiles[0] * 128, tiles[0] * 128 + n * 128)

    @pl.when(p == 0)
    def _():
        t_ref[...] = jnp.concatenate(split(stencil_t(ti_ref[...], tw_ref[...], NT1, even_odd)), axis=0)
        for ref, shift in ((pe_ref, 0), (po_ref, 64)):
            m = jnp.transpose(stencil_t(pi_ref[:, columns], pw_ref[:, columns], 256, lambda a: a + shift))
            hi, lo = split(m)
            ref[...] = jnp.concatenate([hi, hi, lo], axis=0)

    for part in range(2):
        for j in range(n):
            for r in range(3):
                base = p * box + part * half + j * 3 + r
                for zh in range(2):
                    v = x_ref[pl.ds(zh * 32 * rows + base, 32, stride=rows), :]
                    in_ref[2 * j + part, pl.ds(3 * zh + r, 32, stride=6), :] = v

    for k in range(8):
        o = oct_ref[p, k]
        for j in range(n):
            re, im = in_ref[2 * j], in_ref[2 * j + 1]
            c = cos_ref[o, :, j * 128 : j * 128 + 128]
            s = sin_ref[o, :, j * 128 : j * 128 + 128]
            hi, lo = split(jnp.concatenate([re * c + im * s, im * c - re * s], axis=1))
            g = dot(t_ref[...], hi)
            z = g[:NT1] + g[NT1:] + dot(t_ref[:NT1], lo)
            hi, lo = split(z)
            for part in range(2):
                for odd in range(2):
                    for base, v in ((0, hi), (n * 128, lo), (n * 256, hi)):
                        row = (k * 2 + part) * 48
                        z3_ref[odd, row : row + 48, base + j * 128 : base + j * 128 + 128] = v[
                            odd * 48 : odd * 48 + 48, part * 128 : part * 128 + 128
                        ]

    for first in range(0, 8, 4):
        span = slice(first * 96, first * 96 + 384)
        even = dot(z3_ref[0, span, :], pe_ref[...])
        odd = dot(z3_ref[1, span, :], po_ref[...])
        blocks = (even[:, :128], even[:, 128:] + odd[:, :128], odd[:, 128:])
        for k in range(4):
            for part in range(2):
                at = (k * 2 + part) * 48
                for tile in range(3):
                    to = pl.ds((first + k) * 288 + 2 * tile + part, 48, stride=6)
                    v = blocks[tile][at : at + 48]
                    out_ref[to, :] = v + before_ref[0][to, :] if before_ref else v


def whole(shape):
    return pl.BlockSpec(shape, lambda *_: (0,) * len(shape))


VMEM = pl.BlockSpec(memory_space=pltpu.VMEM)
SMEM = pl.BlockSpec(memory_space=pltpu.SMEM)
STENCILS = [whole((4, NT2)), whole((4, NT2)), whole((4, NP2)), whole((4, NP2))]
PARAMS = pltpu.CompilerParams(vmem_limit_bytes=60 * 2**20)
CHILDREN = pl.BlockSpec((8 * 288, 128), lambda p: (p, 0))


def cost(flops, nbytes):
    return pl.CostEstimate(flops=flops, bytes_accessed=nbytes, transcendentals=0)


def table_of(tiles):
    n = len(tiles)
    return pl.BlockSpec((8, NT2, 128 * n), lambda p: (0, 0, tiles[0] // n))


def aggregate(tiles, tables):
    n, _, _, rows = shape_of(tiles)
    table = (8, NT2, NP2)
    part = (8, NT2, 128 * n)
    shapes = [jax.ShapeDtypeStruct((CHIPS * rows, 128), F32)]
    specs = [whole((CHIPS * rows, 128))]
    trig = []
    if tables:
        shapes += [jax.ShapeDtypeStruct(table, F32)] * 2
        specs += [whole(table)] * 2
    else:
        trig = [pltpu.VMEM(part, F32)] * 2
    return pl.pallas_call(
        functools.partial(aggregate_kernel, tiles, tables),
        grid=(PARENTS,),
        in_specs=[SMEM, CHILDREN, whole(table) if tables else table_of(tiles), *STENCILS],
        out_specs=specs,
        out_shape=shapes,
        scratch_shapes=trig
        + [
            pltpu.VMEM((NT2, 288), BF16),
            pltpu.VMEM((2, 256, 128 * n), BF16),
            pltpu.VMEM((2, 256, 128 * n), BF16),
            pltpu.VMEM((768, 384), BF16),
            pltpu.VMEM((768, 384), BF16),
            pltpu.VMEM((8, 288, 256 * n), BF16),
            pltpu.VMEM((2 * n, NT2, 128), F32),
        ],
        compiler_params=PARAMS,
        cost_estimate=cost(n * 4 * 10**9, 10**7),
        name=f"aggregate{n}",
    )


def operators():
    return pl.pallas_call(
        operators_kernel,
        in_specs=[SMEM, VMEM],
        out_specs=[VMEM, VMEM],
        out_shape=[jax.ShapeDtypeStruct((NDISP * SLOT, 128), F32)] * 2,
        compiler_params=PARAMS,
        cost_estimate=cost(10**6, 10**7),
        name="operators",
    )


def translate(tiles):
    n, _, _, rows = shape_of(tiles)
    return pl.pallas_call(
        functools.partial(translate_kernel, tiles),
        in_specs=[SMEM, SMEM, VMEM, VMEM, VMEM],
        out_specs=VMEM,
        out_shape=jax.ShapeDtypeStruct((CHIPS * rows, 128), F32),
        scratch_shapes=[pltpu.VMEM((512 * 16, 128), F32)],
        compiler_params=PARAMS,
        cost_estimate=cost(10**8, 10**7),
        name=f"translate{n}",
    )


def disaggregate(tiles, more):
    n, _, _, rows = shape_of(tiles)
    return pl.pallas_call(
        functools.partial(disaggregate_kernel, tiles),
        grid=(PARENTS,),
        in_specs=[SMEM, whole((CHIPS * rows, 128)), table_of(tiles), table_of(tiles), *STENCILS] + [CHILDREN] * more,
        out_specs=CHILDREN,
        out_shape=jax.ShapeDtypeStruct((32 * 288, 128), F32),
        scratch_shapes=[
            pltpu.VMEM((2 * NT1, NT2), BF16),
            pltpu.VMEM((384 * n, 256), BF16),
            pltpu.VMEM((384 * n, 256), BF16),
            pltpu.VMEM((2 * n, NT2, 128), F32),
            pltpu.VMEM((2, 768, 384 * n), BF16),
        ],
        compiler_params=PARAMS,
        cost_estimate=cost(n * 4 * 10**9, 10**7),
        name=f"disaggregate{n}",
    )


def exchange(a):
    return lax.all_to_all(a.reshape(CHIPS, -1, 128), CHIP, 0, 0, tiled=True).reshape(a.shape)


def together(*arrays):
    return lax.optimization_barrier(arrays)


def local(
    child_out, child_octant, theta_index, theta_weight, phi_index, phi_weight,
    shift_angle, partner_src, partner_disp, translation,
):
    core = lax.axis_index("c")
    zh = lax.axis_index("zh")
    swap = [(0, 1), (1, 0)]
    x = child_out.reshape(32, 2, 144, 128).transpose(0, 2, 1, 3).reshape(32 * 288, 128)
    stencils = (theta_index.T, theta_weight.T, phi_index.T, phi_weight.T)

    def mine(a):
        return lax.dynamic_index_in_dim(a.T.reshape(NPART, 2, 2, 128), core, 2, keepdims=False).reshape(-1)

    src = mine(partner_src)
    holder, p = src // 4, src % 4
    far = jnp.where((holder // 32) % 2 == core, 0, 1)
    src_at = ((far * CHIPS + (holder // 64) * 32 + holder % 32) * PARENTS + p) * SLOT
    disp_at = mine(partner_disp) * SLOT
    ops, = together(translation.transpose(0, 2, 1, 3).reshape(NDISP * 6, 2, NP2))
    ops = ops.reshape(NDISP * 6, 2, 3, 128).transpose(0, 2, 1, 3).reshape(NDISP * 36, 128)

    (out1,) = aggregate(FIRST, False)(child_octant, x, shift_angle, *stencils)
    got1 = exchange(out1)
    x2, _ = together(x, out1)
    out2, cosine, sine = aggregate(SECOND, True)(child_octant, x2, shift_angle, *stencils)
    ops1, ops2 = operators()(zh.reshape(1), ops)
    got1, out2, ops1, ops2, src_at, disp_at = together(got1, out2, ops1, ops2, src_at, disp_at)

    got2 = exchange(out2)
    other1 = lax.ppermute(got1, "c", swap)
    in1 = translate(FIRST)(src_at, disp_at, got1, other1, ops1)
    in1, got2 = together(in1, got2)

    back1 = exchange(in1)
    other2 = lax.ppermute(got2, "c", swap)
    in2 = translate(SECOND)(src_at, disp_at, got2, other2, ops2)
    in2, back1 = together(in2, back1)

    back2 = exchange(in2)
    y = disaggregate(FIRST, 0)(child_octant, back1, cosine, sine, *stencils)
    y, back2 = together(y, back2)
    y = disaggregate(SECOND, 1)(child_octant, back2, cosine, sine, *stencils, y)
    return y.reshape(32, 144, 2, 128).transpose(0, 2, 1, 3).reshape(32, 2, NT1 * NP1)


def solution(mesh):
    fine = Mesh(mesh.devices.reshape(2, 2, 2, 4, 4), ALL)
    boxes = P(ALL)
    in_specs = (boxes, boxes, P(), P(), P(), P(), P(), P(), P(), P(None, None, ("zl", "y", "x"), None))
    return jax.shard_map(local, mesh=fine, in_specs=in_specs, out_specs=boxes, check_vma=False)
```

```python
import functools

import jax
import jax.numpy as jnp
import numpy as np
from jax import lax
from jax.experimental import pallas as pl
from jax.experimental.pallas import tpu as pltpu
from jax.sharding import Mesh, PartitionSpec as P

NT1, NP1, NT2, NP2 = 96, 192, 192, 384
NDISP, NPART = 316, 32
CHIPS = 64
PARENTS = 4
BOXES = CHIPS * PARENTS
SLOT = 16
FIRST, SECOND = (0, 1), (2,)
F32, BF16 = jnp.float32, jnp.bfloat16
ALL = ("zh", "c", "zl", "y", "x")
CHIP = ("zh", "zl", "y", "x")


def fit(fn, powers):
    h = 0.7855 * (1 - np.cos(np.pi * (np.arange(400) + 0.5) / 400))
    a = np.stack([h**k for k in powers], 1)
    return [float(v) for v in np.linalg.lstsq(a, fn(h), rcond=None)[0]]


SIN = fit(np.sin, (1, 3, 5, 7, 9, 11))
COS = fit(np.cos, (0, 2, 4, 6, 8, 10))


def horner(z, coefs):
    r = jnp.full_like(z, coefs[-1])
    for c in coefs[-2::-1]:
        r = r * z + c
    return r


def split(x):
    hi = x.astype(BF16)
    return hi, (x - hi.astype(F32)).astype(BF16)


def dot(a, b):
    return jnp.dot(a, b, preferred_element_type=F32)


def stencil_t(index, weight, rows, target):
    n = index.shape[1]
    row = lax.broadcasted_iota(jnp.int32, (rows, n), 0)
    out = jnp.zeros((rows, n), F32)
    for j in range(4):
        out = out + jnp.where(row == target(index[j : j + 1, :]), weight[j : j + 1, :], 0.0)
    return out


def even_odd(a):
    return jnp.where(a % 2 == 0, a // 2, 48 + a // 2)


def shape_of(tiles):
    n = len(tiles)
    return n, 3 * n, 6 * n, 24 * n


def aggregate_kernel(tiles, tables, oct_ref, x_ref, angle_ref, ti_ref, tw_ref, pi_ref, pw_ref, out_ref, cos_ref, sin_ref, *scratch):
    t3_ref, pe_ref, po_ref, vh_ref, vl_ref, y3_ref, acc_ref = scratch
    n, half, box, rows = shape_of(tiles)
    p = pl.program_id(0)
    first = tiles[0] if tables else 0
    columns = slice(tiles[0] * 128, tiles[0] * 128 + n * 128)

    @pl.when(p == 0)
    def _():
        def trig(o, _):
            for r in range(0, NT2, 48):
                h = angle_ref[o, r : r + 48, :] * 0.5
                z = h * h
                s = horner(z, SIN) * h
                c = horner(z, COS)
                cos_ref[o, r : r + 48, :] = 1.0 - 2.0 * (s * s)
                sin_ref[o, r : r + 48, :] = 2.0 * (s * c)
            return 0

        lax.fori_loop(0, 8, trig, 0)
        tt = stencil_t(ti_ref[...], tw_ref[...], 128, even_odd)
        t = jnp.transpose(jnp.concatenate([tt, jnp.zeros((128, 64), F32)], axis=1))[:NT2, :NT1]
        hi, lo = split(t)
        t3_ref[...] = jnp.concatenate([hi, hi, lo], axis=1)
        for ref, shift in ((pe_ref, 0), (po_ref, 64)):
            hi, lo = split(stencil_t(pi_ref[:, columns], pw_ref[:, columns], 256, lambda a: a + shift))
            ref[0], ref[1] = hi, lo

    for k in range(8):
        for part in range(2):
            row = (k * 2 + part) * 48
            for tile in range(3):
                v = x_ref[pl.ds(k * 288 + 2 * tile + part, 48, stride=6), :]
                hi, lo = split(v)
                vh_ref[row : row + 48, tile * 128 : tile * 128 + 128] = hi
                vl_ref[row : row + 48, tile * 128 : tile * 128 + 128] = lo
    for odd, ref in ((0, pe_ref), (1, po_ref)):
        cols = slice(odd * 128, odd * 128 + 256)
        for m in range(0, 768, 192):
            vh, vl = vh_ref[m : m + 192, cols], vl_ref[m : m + 192, cols]
            y = dot(vh, ref[0]) + dot(vl, ref[0]) + dot(vh, ref[1])
            yh, yl = split(y)
            for kk in range(2):
                for part in range(2):
                    r = (kk * 2 + part) * 48
                    for j in range(n):
                        col = j * 256 + part * 128
                        for base, v in ((0, yh), (96, yl), (192, yh)):
                            y3_ref[m // 96 + kk, base + odd * 48 : base + odd * 48 + 48, col : col + 128] = v[
                                r : r + 48, j * 128 : j * 128 + 128
                            ]

    for k in range(8):
        o = oct_ref[p, k]
        for j in range(n):
            f = dot(t3_ref[...], y3_ref[k, :, j * 256 : j * 256 + 256])
            re, im = f[:, :128], f[:, 128:]
            at = (first + j) * 128
            c = cos_ref[o, :, at : at + 128]
            s = sin_ref[o, :, at : at + 128]
            if k == 0:
                acc_ref[2 * j] = re * c - im * s
                acc_ref[2 * j + 1] = re * s + im * c
            else:
                acc_ref[2 * j] += re * c - im * s
                acc_ref[2 * j + 1] += re * s + im * c

    for part in range(2):
        for j in range(n):
            for r in range(3):
                base = p * box + part * half + j * 3 + r
                for zh in range(2):
                    v = acc_ref[2 * j + part, pl.ds(3 * zh + r, 32, stride=6), :]
                    out_ref[pl.ds(zh * 32 * rows + base, 32, stride=rows), :] = v


def operators_kernel(zh_ref, t_ref, first_ref, second_ref):
    half = zh_ref[0] * 18

    def one(d, _):
        for ref, tiles in ((first_ref, FIRST), (second_ref, SECOND)):
            gap = 8 if len(tiles) == 2 else 3
            for part in range(2):
                for jj, j in enumerate(tiles):
                    v = t_ref[pl.ds(d * 36 + half + j * 2 + part, 3, stride=6), :]
                    ref[pl.ds(d * SLOT + part * gap + jj * 3, 3), :] = v
        return 0

    lax.fori_loop(0, NDISP, one, 0, unroll=4)


def translate_kernel(tiles, src_ref, disp_ref, own_ref, other_ref, t_ref, out_ref, s_ref):
    n, half, box, rows = shape_of(tiles)

    def lay(i, _):
        for first, ref in ((0, own_ref), (CHIPS, other_ref)):
            for p in range(PARENTS):
                re = ref[pl.ds(i * rows + p * box, half), :]
                im = ref[pl.ds(i * rows + p * box + half, half), :]
                to = ((first + i) * PARENTS + p) * 16
                s_ref[pl.ds(to, half), :] = re
                s_ref[pl.ds(to + 8, half), :] = im
                if n == 1:
                    s_ref[pl.ds(to + 3, half), :] = im
                    s_ref[pl.ds(to + 11, half), :] = re
        return 0

    lax.fori_loop(0, CHIPS, lay, 0, unroll=2)

    def receiver(i, _):
        sums = None
        for q in range(NPART):
            a = pl.multiple_of(src_ref.at[pl.ds(q * BOXES, BOXES)][i], 8)
            d = pl.multiple_of(disp_ref.at[pl.ds(q * BOXES, BOXES)][i], 8)
            s0, s1 = s_ref[pl.ds(a, 8), :], s_ref[pl.ds(a + 8, 8), :]
            t0 = t_ref[pl.ds(d, 8), :]
            if n == 1:
                terms = (t0 * s0, t0 * s1)
            else:
                t1 = t_ref[pl.ds(d + 8, 8), :]
                terms = (t0 * s0, t1 * s1, t0 * s1, t1 * s0)
            sums = terms if q == 0 else tuple(x + y for x, y in zip(sums, terms))
        if n == 1:
            re, im = sums[0][0:3] - sums[0][3:6], sums[1][0:3] + sums[1][3:6]
        else:
            re, im = (sums[0] - sums[1])[:half], (sums[2] + sums[3])[:half]
        to = (i // PARENTS) * rows + (i % PARENTS) * box
        out_ref[pl.ds(to, half), :] = re
        out_ref[pl.ds(to + half, half), :] = im
        return 0

    lax.fori_loop(0, CHIPS * PARENTS, receiver, 0, unroll=2)


def disaggregate_kernel(tiles, oct_ref, x_ref, cos_ref, sin_ref, ti_ref, tw_ref, pi_ref, pw_ref, *rest):
    (*before_ref, out_ref, t_ref, pe_ref, po_ref, in_ref, z3_ref) = rest
    n, half, box, rows = shape_of(tiles)
    p = pl.program_id(0)
    columns = slice(tiles[0] * 128, tiles[0] * 128 + n * 128)

    @pl.when(p == 0)
    def _():
        t_ref[...] = jnp.concatenate(split(stencil_t(ti_ref[...], tw_ref[...], NT1, even_odd)), axis=0)
        for ref, shift in ((pe_ref, 0), (po_ref, 64)):
            m = jnp.transpose(stencil_t(pi_ref[:, columns], pw_ref[:, columns], 256, lambda a: a + shift))
            hi, lo = split(m)
            ref[...] = jnp.concatenate([hi, hi, lo], axis=0)

    for part in range(2):
        for j in range(n):
            for r in range(3):
                base = p * box + part * half + j * 3 + r
                for zh in range(2):
                    v = x_ref[pl.ds(zh * 32 * rows + base, 32, stride=rows), :]
                    in_ref[2 * j + part, pl.ds(3 * zh + r, 32, stride=6), :] = v

    for k in range(8):
        o = oct_ref[p, k]
        for j in range(n):
            re, im = in_ref[2 * j], in_ref[2 * j + 1]
            c = cos_ref[o, :, j * 128 : j * 128 + 128]
            s = sin_ref[o, :, j * 128 : j * 128 + 128]
            hi, lo = split(jnp.concatenate([re * c + im * s, im * c - re * s], axis=1))
            g = dot(t_ref[...], hi)
            z = g[:NT1] + g[NT1:] + dot(t_ref[:NT1], lo)
            hi, lo = split(z)
            for part in range(2):
                for odd in range(2):
                    for base, v in ((0, hi), (n * 128, lo), (n * 256, hi)):
                        row = (k * 2 + part) * 48
                        z3_ref[odd, row : row + 48, base + j * 128 : base + j * 128 + 128] = v[
                            odd * 48 : odd * 48 + 48, part * 128 : part * 128 + 128
                        ]

    for first in range(0, 8, 4):
        span = slice(first * 96, first * 96 + 384)
        even = dot(z3_ref[0, span, :], pe_ref[...])
        odd = dot(z3_ref[1, span, :], po_ref[...])
        blocks = (even[:, :128], even[:, 128:] + odd[:, :128], odd[:, 128:])
        for k in range(4):
            for part in range(2):
                at = (k * 2 + part) * 48
                for tile in range(3):
                    to = pl.ds((first + k) * 288 + 2 * tile + part, 48, stride=6)
                    v = blocks[tile][at : at + 48]
                    out_ref[to, :] = v + before_ref[0][to, :] if before_ref else v


def whole(shape):
    return pl.BlockSpec(shape, lambda *_: (0,) * len(shape))


VMEM = pl.BlockSpec(memory_space=pltpu.VMEM)
SMEM = pl.BlockSpec(memory_space=pltpu.SMEM)
STENCILS = [whole((4, NT2)), whole((4, NT2)), whole((4, NP2)), whole((4, NP2))]
PARAMS = pltpu.CompilerParams(vmem_limit_bytes=52 * 2**20)
ROOMY = pltpu.CompilerParams(vmem_limit_bytes=60 * 2**20)
CHILDREN = pl.BlockSpec((8 * 288, 128), lambda p: (p, 0))


def cost(flops, nbytes):
    return pl.CostEstimate(flops=flops, bytes_accessed=nbytes, transcendentals=0)


def table_of(tiles):
    n = len(tiles)
    return pl.BlockSpec((8, NT2, 128 * n), lambda p: (0, 0, tiles[0] // n))


def aggregate(tiles, tables):
    n, _, _, rows = shape_of(tiles)
    table = (8, NT2, NP2)
    part = (8, NT2, 128 * n)
    shapes = [jax.ShapeDtypeStruct((CHIPS * rows, 128), F32)]
    specs = [whole((CHIPS * rows, 128))]
    trig = []
    if tables:
        shapes += [jax.ShapeDtypeStruct(table, F32)] * 2
        specs += [whole(table)] * 2
    else:
        trig = [pltpu.VMEM(part, F32)] * 2
    return pl.pallas_call(
        functools.partial(aggregate_kernel, tiles, tables),
        grid=(PARENTS,),
        in_specs=[SMEM, CHILDREN, whole(table) if tables else table_of(tiles), *STENCILS],
        out_specs=specs,
        out_shape=shapes,
        scratch_shapes=trig
        + [
            pltpu.VMEM((NT2, 288), BF16),
            pltpu.VMEM((2, 256, 128 * n), BF16),
            pltpu.VMEM((2, 256, 128 * n), BF16),
            pltpu.VMEM((768, 384), BF16),
            pltpu.VMEM((768, 384), BF16),
            pltpu.VMEM((8, 288, 256 * n), BF16),
            pltpu.VMEM((2 * n, NT2, 128), F32),
        ],
        compiler_params=ROOMY,
        cost_estimate=cost(n * 4 * 10**9, 10**7),
        name=f"aggregate{n}",
    )


def operators():
    return pl.pallas_call(
        operators_kernel,
        in_specs=[SMEM, VMEM],
        out_specs=[VMEM, VMEM],
        out_shape=[jax.ShapeDtypeStruct((NDISP * SLOT, 128), F32)] * 2,
        compiler_params=ROOMY,
        cost_estimate=cost(10**6, 10**7),
        name="operators",
    )


def translate(tiles):
    n, _, _, rows = shape_of(tiles)
    return pl.pallas_call(
        functools.partial(translate_kernel, tiles),
        in_specs=[SMEM, SMEM, VMEM, VMEM, VMEM],
        out_specs=VMEM,
        out_shape=jax.ShapeDtypeStruct((CHIPS * rows, 128), F32),
        scratch_shapes=[pltpu.VMEM((512 * 16, 128), F32)],
        compiler_params=PARAMS,
        cost_estimate=cost(10**8, 10**7),
        name=f"translate{n}",
    )


def disaggregate(tiles, more):
    n, _, _, rows = shape_of(tiles)
    return pl.pallas_call(
        functools.partial(disaggregate_kernel, tiles),
        grid=(PARENTS,),
        in_specs=[SMEM, whole((CHIPS * rows, 128)), table_of(tiles), table_of(tiles), *STENCILS] + [CHILDREN] * more,
        out_specs=CHILDREN,
        out_shape=jax.ShapeDtypeStruct((32 * 288, 128), F32),
        scratch_shapes=[
            pltpu.VMEM((2 * NT1, NT2), BF16),
            pltpu.VMEM((384 * n, 256), BF16),
            pltpu.VMEM((384 * n, 256), BF16),
            pltpu.VMEM((2 * n, NT2, 128), F32),
            pltpu.VMEM((2, 768, 384 * n), BF16),
        ],
        compiler_params=PARAMS,
        cost_estimate=cost(n * 4 * 10**9, 10**7),
        name=f"disaggregate{n}",
    )


def exchange(a):
    return lax.all_to_all(a.reshape(CHIPS, -1, 128), CHIP, 0, 0, tiled=True).reshape(a.shape)


def together(*arrays):
    return lax.optimization_barrier(arrays)


def local(
    child_out, child_octant, theta_index, theta_weight, phi_index, phi_weight,
    shift_angle, partner_src, partner_disp, translation,
):
    core = lax.axis_index("c")
    zh = lax.axis_index("zh")
    swap = [(0, 1), (1, 0)]
    x = child_out.reshape(32, 2, 144, 128).transpose(0, 2, 1, 3).reshape(32 * 288, 128)
    stencils = (theta_index.T, theta_weight.T, phi_index.T, phi_weight.T)

    def mine(a):
        return lax.dynamic_index_in_dim(a.T.reshape(NPART, 2, 2, 128), core, 2, keepdims=False).reshape(-1)

    src = mine(partner_src)
    holder, p = src // 4, src % 4
    far = jnp.where((holder // 32) % 2 == core, 0, 1)
    src_at = ((far * CHIPS + (holder // 64) * 32 + holder % 32) * PARENTS + p) * SLOT
    disp_at = mine(partner_disp) * SLOT
    ops, = together(translation.transpose(0, 2, 1, 3).reshape(NDISP * 6, 2, NP2))
    ops = ops.reshape(NDISP * 6, 2, 3, 128).transpose(0, 2, 1, 3).reshape(NDISP * 36, 128)

    (out1,) = aggregate(FIRST, False)(child_octant, x, shift_angle, *stencils)
    got1 = exchange(out1)
    x2, _ = together(x, out1)
    out2, cosine, sine = aggregate(SECOND, True)(child_octant, x2, shift_angle, *stencils)
    ops1, ops2 = operators()(zh.reshape(1), ops)
    got1, out2, ops1, ops2, src_at, disp_at = together(got1, out2, ops1, ops2, src_at, disp_at)

    got2 = exchange(out2)
    other1 = lax.ppermute(got1, "c", swap)
    in1 = translate(FIRST)(src_at, disp_at, got1, other1, ops1)
    in1, got2 = together(in1, got2)

    back1 = exchange(in1)
    other2 = lax.ppermute(got2, "c", swap)
    in2 = translate(SECOND)(src_at, disp_at, got2, other2, ops2)
    in2, back1 = together(in2, back1)

    back2 = exchange(in2)
    y = disaggregate(FIRST, 0)(child_octant, back1, cosine, sine, *stencils)
    y, back2 = together(y, back2)
    y = disaggregate(SECOND, 1)(child_octant, back2, cosine, sine, *stencils, y)
    return y.reshape(32, 144, 2, 128).transpose(0, 2, 1, 3).reshape(32, 2, NT1 * NP1)


def solution(mesh):
    fine = Mesh(mesh.devices.reshape(2, 2, 2, 4, 4), ALL)
    boxes = P(ALL)
    in_specs = (boxes, boxes, P(), P(), P(), P(), P(), P(), P(), P(None, None, ("zl", "y", "x"), None))
    return jax.shard_map(local, mesh=fine, in_specs=in_specs, out_specs=boxes, check_vma=False)
```

```python
import functools

import jax
import jax.numpy as jnp
import numpy as np
from jax import lax
from jax.experimental import pallas as pl
from jax.experimental.pallas import tpu as pltpu
from jax.sharding import Mesh, PartitionSpec as P

NT1, NP1, NT2, NP2 = 96, 192, 192, 384
NDISP, NPART = 316, 32
CHIPS = 64
PARENTS = 4
BOXES = CHIPS * PARENTS
SLOT = 16
FIRST, SECOND = (0, 1), (2,)
F32, BF16 = jnp.float32, jnp.bfloat16
ALL = ("zh", "c", "zl", "y", "x")
CHIP = ("zh", "zl", "y", "x")


def fit(fn, powers):
    h = 0.7855 * (1 - np.cos(np.pi * (np.arange(400) + 0.5) / 400))
    a = np.stack([h**k for k in powers], 1)
    return [float(v) for v in np.linalg.lstsq(a, fn(h), rcond=None)[0]]


SIN = fit(np.sin, (1, 3, 5, 7, 9))
COS = fit(np.cos, (0, 2, 4, 6, 8, 10))


def horner(z, coefs):
    r = jnp.full_like(z, coefs[-1])
    for c in coefs[-2::-1]:
        r = r * z + c
    return r


def split(x):
    hi = x.astype(BF16)
    return hi, (x - hi.astype(F32)).astype(BF16)


def dot(a, b):
    return jnp.dot(a, b, preferred_element_type=F32)


def stencil_t(index, weight, rows, target):
    n = index.shape[1]
    row = lax.broadcasted_iota(jnp.int32, (rows, n), 0)
    out = jnp.zeros((rows, n), F32)
    for j in range(4):
        out = out + jnp.where(row == target(index[j : j + 1, :]), weight[j : j + 1, :], 0.0)
    return out


def even_odd(a):
    return jnp.where(a % 2 == 0, a // 2, 48 + a // 2)


def shape_of(tiles):
    n = len(tiles)
    return n, 3 * n, 6 * n, 24 * n


def aggregate_kernel(tiles, tables, oct_ref, x_ref, angle_ref, ti_ref, tw_ref, pi_ref, pw_ref, out_ref, cos_ref, sin_ref, *scratch):
    t3_ref, pe_ref, po_ref, vh_ref, vl_ref, y3_ref, acc_ref = scratch
    n, half, box, rows = shape_of(tiles)
    p = pl.program_id(0)
    first = tiles[0] if tables else 0
    columns = slice(tiles[0] * 128, tiles[0] * 128 + n * 128)

    @pl.when(p == 0)
    def _():
        def trig(o, _):
            for r in range(0, NT2, 48):
                h = angle_ref[o, r : r + 48, :] * 0.5
                z = h * h
                s = horner(z, SIN) * h
                c = horner(z, COS)
                cos_ref[o, r : r + 48, :] = 1.0 - 2.0 * (s * s)
                sin_ref[o, r : r + 48, :] = 2.0 * (s * c)
            return 0

        lax.fori_loop(0, 8, trig, 0)
        tt = stencil_t(ti_ref[...], tw_ref[...], 128, even_odd)
        t = jnp.transpose(jnp.concatenate([tt, jnp.zeros((128, 64), F32)], axis=1))[:NT2, :NT1]
        hi, lo = split(t)
        t3_ref[...] = jnp.concatenate([hi, hi, lo], axis=1)
        for ref, shift in ((pe_ref, 0), (po_ref, 64)):
            hi, lo = split(stencil_t(pi_ref[:, columns], pw_ref[:, columns], 256, lambda a: a + shift))
            ref[0], ref[1] = hi, lo

    for k in range(8):
        for part in range(2):
            row = (k * 2 + part) * 48
            for tile in range(3):
                v = x_ref[pl.ds(k * 288 + 2 * tile + part, 48, stride=6), :]
                hi, lo = split(v)
                vh_ref[row : row + 48, tile * 128 : tile * 128 + 128] = hi
                vl_ref[row : row + 48, tile * 128 : tile * 128 + 128] = lo
    for odd, ref in ((0, pe_ref), (1, po_ref)):
        cols = slice(odd * 128, odd * 128 + 256)
        for m in range(0, 768, 192):
            vh, vl = vh_ref[m : m + 192, cols], vl_ref[m : m + 192, cols]
            y = dot(vh, ref[0]) + dot(vl, ref[0]) + dot(vh, ref[1])
            yh, yl = split(y)
            for kk in range(2):
                for part in range(2):
                    r = (kk * 2 + part) * 48
                    for j in range(n):
                        col = j * 256 + part * 128
                        for base, v in ((0, yh), (96, yl)):
                            y3_ref[m // 96 + kk, base + odd * 48 : base + odd * 48 + 48, col : col + 128] = v[
                                r : r + 48, j * 128 : j * 128 + 128
                            ]

    for k in range(8):
        o = oct_ref[p, k]
        for j in range(n):
            y = y3_ref[k, :, j * 256 : j * 256 + 256]
            f = dot(t3_ref[:, :192], y) + dot(t3_ref[:, 192:], y[:96])
            re, im = f[:, :128], f[:, 128:]
            at = (first + j) * 128
            c = cos_ref[o, :, at : at + 128]
            s = sin_ref[o, :, at : at + 128]
            if k == 0:
                acc_ref[2 * j] = re * c - im * s
                acc_ref[2 * j + 1] = re * s + im * c
            else:
                acc_ref[2 * j] += re * c - im * s
                acc_ref[2 * j + 1] += re * s + im * c

    for part in range(2):
        for j in range(n):
            for r in range(3):
                base = p * box + part * half + j * 3 + r
                for zh in range(2):
                    v = acc_ref[2 * j + part, pl.ds(3 * zh + r, 32, stride=6), :]
                    out_ref[pl.ds(zh * 32 * rows + base, 32, stride=rows), :] = v


def operators_kernel(zh_ref, t_ref, first_ref, second_ref):
    half = zh_ref[0] * 18

    def one(d, _):
        for ref, tiles, slot, gap in ((first_ref, FIRST, SLOT, 8), (second_ref, SECOND, SLOT // 2, 3)):
            for part in range(2):
                for jj, j in enumerate(tiles):
                    v = t_ref[pl.ds(d * 36 + half + j * 2 + part, 3, stride=6), :]
                    ref[pl.ds(d * slot + part * gap + jj * 3, 3), :] = v
        return 0

    lax.fori_loop(0, NDISP, one, 0, unroll=4)


def translate_kernel(tiles, src_ref, disp_ref, own_ref, other_ref, t_ref, out_ref, s_ref):
    n, half, box, rows = shape_of(tiles)

    def lay(i, _):
        for first, ref in ((0, own_ref), (CHIPS, other_ref)):
            for p in range(PARENTS):
                re = ref[pl.ds(i * rows + p * box, half), :]
                im = ref[pl.ds(i * rows + p * box + half, half), :]
                to = ((first + i) * PARENTS + p) * 16
                s_ref[pl.ds(to, half), :] = re
                s_ref[pl.ds(to + 8, half), :] = im
                if n == 1:
                    s_ref[pl.ds(to + 3, half), :] = im
                    s_ref[pl.ds(to + 11, half), :] = re
        return 0

    lax.fori_loop(0, CHIPS, lay, 0, unroll=4)

    def receiver(i, _):
        sums = None
        for q in range(NPART):
            a = pl.multiple_of(src_ref.at[pl.ds(q * BOXES, BOXES)][i], 8)
            d = pl.multiple_of(disp_ref.at[pl.ds(q * BOXES, BOXES)][i], 8)
            s0, s1 = s_ref[pl.ds(a, 8), :], s_ref[pl.ds(a + 8, 8), :]
            t0 = t_ref[pl.ds(d, 8), :]
            if n == 1:
                terms = (t0 * s0, t0 * s1)
            else:
                t1 = t_ref[pl.ds(d + 8, 8), :]
                terms = (t0 * s0, t1 * s1, t0 * s1, t1 * s0)
            sums = terms if q == 0 else tuple(x + y for x, y in zip(sums, terms))
        if n == 1:
            re, im = sums[0][0:3] - sums[0][3:6], sums[1][0:3] + sums[1][3:6]
        else:
            re, im = (sums[0] - sums[1])[:half], (sums[2] + sums[3])[:half]
        to = (i // PARENTS) * rows + (i % PARENTS) * box
        out_ref[pl.ds(to, half), :] = re
        out_ref[pl.ds(to + half, half), :] = im
        return 0

    lax.fori_loop(0, CHIPS * PARENTS, receiver, 0, unroll=4)


def disaggregate_kernel(tiles, oct_ref, x_ref, cos_ref, sin_ref, ti_ref, tw_ref, pi_ref, pw_ref, *rest):
    (*before_ref, out_ref, t_ref, pe_ref, po_ref, in_ref, z3_ref) = rest
    n, half, box, rows = shape_of(tiles)
    p = pl.program_id(0)
    columns = slice(tiles[0] * 128, tiles[0] * 128 + n * 128)

    @pl.when(p == 0)
    def _():
        t_ref[...] = jnp.concatenate(split(stencil_t(ti_ref[...], tw_ref[...], NT1, even_odd)), axis=0)
        for ref, shift in ((pe_ref, 0), (po_ref, 64)):
            m = jnp.transpose(stencil_t(pi_ref[:, columns], pw_ref[:, columns], 256, lambda a: a + shift))
            hi, lo = split(m)
            ref[...] = jnp.concatenate([hi, hi, lo], axis=0)

    for part in range(2):
        for j in range(n):
            for r in range(3):
                base = p * box + part * half + j * 3 + r
                for zh in range(2):
                    v = x_ref[pl.ds(zh * 32 * rows + base, 32, stride=rows), :]
                    in_ref[2 * j + part, pl.ds(3 * zh + r, 32, stride=6), :] = v

    for k in range(8):
        o = oct_ref[p, k]
        for j in range(n):
            re, im = in_ref[2 * j], in_ref[2 * j + 1]
            c = cos_ref[o, :, j * 128 : j * 128 + 128]
            s = sin_ref[o, :, j * 128 : j * 128 + 128]
            hi, lo = split(jnp.concatenate([re * c + im * s, im * c - re * s], axis=1))
            g = dot(t_ref[...], hi)
            z = g[:NT1] + g[NT1:] + dot(t_ref[:NT1], lo)
            hi, lo = split(z)
            for part in range(2):
                for odd in range(2):
                    for base, v in ((0, hi), (n * 128, lo), (n * 256, hi)):
                        row = (k * 2 + part) * 48
                        z3_ref[odd, row : row + 48, base + j * 128 : base + j * 128 + 128] = v[
                            odd * 48 : odd * 48 + 48, part * 128 : part * 128 + 128
                        ]

    for first in range(0, 8, 4):
        span = slice(first * 96, first * 96 + 384)
        even = dot(z3_ref[0, span, :], pe_ref[...])
        odd = dot(z3_ref[1, span, :], po_ref[...])
        blocks = (even[:, :128], even[:, 128:] + odd[:, :128], odd[:, 128:])
        for k in range(4):
            for part in range(2):
                at = (k * 2 + part) * 48
                for tile in range(3):
                    to = pl.ds((first + k) * 288 + 2 * tile + part, 48, stride=6)
                    v = blocks[tile][at : at + 48]
                    out_ref[to, :] = v + before_ref[0][to, :] if before_ref else v


def whole(shape):
    return pl.BlockSpec(shape, lambda *_: (0,) * len(shape))


VMEM = pl.BlockSpec(memory_space=pltpu.VMEM)
SMEM = pl.BlockSpec(memory_space=pltpu.SMEM)
STENCILS = [whole((4, NT2)), whole((4, NT2)), whole((4, NP2)), whole((4, NP2))]
PARAMS = pltpu.CompilerParams(vmem_limit_bytes=52 * 2**20)
ROOMY = pltpu.CompilerParams(vmem_limit_bytes=60 * 2**20)
CHILDREN = pl.BlockSpec((8 * 288, 128), lambda p: (p, 0))


def cost(flops, nbytes):
    return pl.CostEstimate(flops=flops, bytes_accessed=nbytes, transcendentals=0)


def table_of(tiles):
    n = len(tiles)
    return pl.BlockSpec((8, NT2, 128 * n), lambda p: (0, 0, tiles[0] // n))


def aggregate(tiles, tables):
    n, _, _, rows = shape_of(tiles)
    table = (8, NT2, NP2)
    part = (8, NT2, 128 * n)
    shapes = [jax.ShapeDtypeStruct((CHIPS * rows, 128), F32)]
    specs = [whole((CHIPS * rows, 128))]
    trig = []
    if tables:
        shapes += [jax.ShapeDtypeStruct(table, F32)] * 2
        specs += [whole(table)] * 2
    else:
        trig = [pltpu.VMEM(part, F32)] * 2
    return pl.pallas_call(
        functools.partial(aggregate_kernel, tiles, tables),
        grid=(PARENTS,),
        in_specs=[SMEM, CHILDREN, whole(table) if tables else table_of(tiles), *STENCILS],
        out_specs=specs,
        out_shape=shapes,
        scratch_shapes=trig
        + [
            pltpu.VMEM((NT2, 288), BF16),
            pltpu.VMEM((2, 256, 128 * n), BF16),
            pltpu.VMEM((2, 256, 128 * n), BF16),
            pltpu.VMEM((768, 384), BF16),
            pltpu.VMEM((768, 384), BF16),
            pltpu.VMEM((8, 192, 256 * n), BF16),
            pltpu.VMEM((2 * n, NT2, 128), F32),
        ],
        compiler_params=ROOMY,
        cost_estimate=cost(n * 4 * 10**9, 10**7),
        name=f"aggregate{n}",
    )


def operators():
    return pl.pallas_call(
        operators_kernel,
        in_specs=[SMEM, VMEM],
        out_specs=[VMEM, VMEM],
        out_shape=[jax.ShapeDtypeStruct((NDISP * slot, 128), F32) for slot in (SLOT, SLOT // 2)],
        compiler_params=ROOMY,
        cost_estimate=cost(10**6, 10**7),
        name="operators",
    )


def translate(tiles):
    n, _, _, rows = shape_of(tiles)
    return pl.pallas_call(
        functools.partial(translate_kernel, tiles),
        in_specs=[SMEM, SMEM, VMEM, VMEM, VMEM],
        out_specs=VMEM,
        out_shape=jax.ShapeDtypeStruct((CHIPS * rows, 128), F32),
        scratch_shapes=[pltpu.VMEM((512 * 16, 128), F32)],
        compiler_params=PARAMS,
        cost_estimate=cost(10**8, 10**7),
        name=f"translate{n}",
    )


def disaggregate(tiles, more):
    n, _, _, rows = shape_of(tiles)
    return pl.pallas_call(
        functools.partial(disaggregate_kernel, tiles),
        grid=(PARENTS,),
        in_specs=[SMEM, whole((CHIPS * rows, 128)), table_of(tiles), table_of(tiles), *STENCILS] + [CHILDREN] * more,
        out_specs=CHILDREN,
        out_shape=jax.ShapeDtypeStruct((32 * 288, 128), F32),
        scratch_shapes=[
            pltpu.VMEM((2 * NT1, NT2), BF16),
            pltpu.VMEM((384 * n, 256), BF16),
            pltpu.VMEM((384 * n, 256), BF16),
            pltpu.VMEM((2 * n, NT2, 128), F32),
            pltpu.VMEM((2, 768, 384 * n), BF16),
        ],
        compiler_params=PARAMS,
        cost_estimate=cost(n * 4 * 10**9, 10**7),
        name=f"disaggregate{n}",
    )


def exchange(a):
    return lax.all_to_all(a.reshape(CHIPS, -1, 128), CHIP, 0, 0, tiled=True).reshape(a.shape)


def together(*arrays):
    return lax.optimization_barrier(arrays)


def local(
    child_out, child_octant, theta_index, theta_weight, phi_index, phi_weight,
    shift_angle, partner_src, partner_disp, translation,
):
    core = lax.axis_index("c")
    zh = lax.axis_index("zh")
    swap = [(0, 1), (1, 0)]
    x = child_out.reshape(32, 2, 144, 128).transpose(0, 2, 1, 3).reshape(32 * 288, 128)
    stencils = (theta_index.T, theta_weight.T, phi_index.T, phi_weight.T)

    def mine(a):
        return lax.dynamic_index_in_dim(a.T.reshape(NPART, 2, 2, 128), core, 2, keepdims=False).reshape(-1)

    src = mine(partner_src)
    holder, p = src // 4, src % 4
    far = jnp.where((holder // 32) % 2 == core, 0, 1)
    src_at = ((far * CHIPS + (holder // 64) * 32 + holder % 32) * PARENTS + p) * SLOT
    disp1 = mine(partner_disp) * SLOT
    disp2 = disp1 // 2
    ops, = together(translation.transpose(0, 2, 1, 3).reshape(NDISP * 6, 2, NP2))
    ops = ops.reshape(NDISP * 6, 2, 3, 128).transpose(0, 2, 1, 3).reshape(NDISP * 36, 128)

    (out1,) = aggregate(FIRST, False)(child_octant, x, shift_angle, *stencils)
    got1 = exchange(out1)
    x2, _ = together(x, out1)
    out2, cosine, sine = aggregate(SECOND, True)(child_octant, x2, shift_angle, *stencils)
    ops1, ops2 = operators()(zh.reshape(1), ops)
    got1, out2, ops1, ops2, src_at, disp1, disp2 = together(got1, out2, ops1, ops2, src_at, disp1, disp2)

    got2 = exchange(out2)
    other1 = lax.ppermute(got1, "c", swap)
    in1 = translate(FIRST)(src_at, disp1, got1, other1, ops1)
    in1, got2 = together(in1, got2)

    back1 = exchange(in1)
    other2 = lax.ppermute(got2, "c", swap)
    in2 = translate(SECOND)(src_at, disp2, got2, other2, ops2)
    in2, back1 = together(in2, back1)

    back2 = exchange(in2)
    y = disaggregate(FIRST, 0)(child_octant, back1, cosine, sine, *stencils)
    y, back2 = together(y, back2)
    y = disaggregate(SECOND, 1)(child_octant, back2, cosine, sine, *stencils, y)
    return y.reshape(32, 144, 2, 128).transpose(0, 2, 1, 3).reshape(32, 2, NT1 * NP1)


def solution(mesh):
    fine = Mesh(mesh.devices.reshape(2, 2, 2, 4, 4), ALL)
    boxes = P(ALL)
    in_specs = (boxes, boxes, P(), P(), P(), P(), P(), P(), P(), P(None, None, ("zl", "y", "x"), None))
    return jax.shard_map(local, mesh=fine, in_specs=in_specs, out_specs=boxes, check_vma=False)
```

```python
import functools

import jax
import jax.numpy as jnp
import numpy as np
from jax import lax
from jax.experimental import pallas as pl
from jax.experimental.pallas import tpu as pltpu
from jax.sharding import Mesh, PartitionSpec as P

NT1, NP1, NT2, NP2 = 96, 192, 192, 384
NDISP, NPART = 316, 32
CHIPS = 64
PARENTS = 4
BOXES = CHIPS * PARENTS
SLOT = 16
FIRST, SECOND = (0, 1), (2,)
F32, BF16 = jnp.float32, jnp.bfloat16
ALL = ("zh", "c", "zl", "y", "x")
CHIP = ("zh", "zl", "y", "x")


def fit(fn, powers):
    h = 0.7855 * (1 - np.cos(np.pi * (np.arange(400) + 0.5) / 400))
    a = np.stack([h**k for k in powers], 1)
    return [float(v) for v in np.linalg.lstsq(a, fn(h), rcond=None)[0]]


SIN = fit(np.sin, (1, 3, 5, 7, 9))
COS = fit(np.cos, (0, 2, 4, 6, 8, 10))


def horner(z, coefs):
    r = jnp.full_like(z, coefs[-1])
    for c in coefs[-2::-1]:
        r = r * z + c
    return r


def split(x):
    hi = x.astype(BF16)
    return hi, (x - hi.astype(F32)).astype(BF16)


def dot(a, b):
    return jnp.dot(a, b, preferred_element_type=F32)


def stencil_t(index, weight, rows, target):
    n = index.shape[1]
    row = lax.broadcasted_iota(jnp.int32, (rows, n), 0)
    out = jnp.zeros((rows, n), F32)
    for j in range(4):
        out = out + jnp.where(row == target(index[j : j + 1, :]), weight[j : j + 1, :], 0.0)
    return out


def even_odd(a):
    return jnp.where(a % 2 == 0, a // 2, 48 + a // 2)


def shape_of(tiles):
    n = len(tiles)
    return n, 3 * n, 6 * n, 24 * n


def aggregate_kernel(tiles, tables, oct_ref, x_ref, angle_ref, ti_ref, tw_ref, pi_ref, pw_ref, out_ref, cos_ref, sin_ref, *scratch):
    t3_ref, pe_ref, po_ref, vh_ref, vl_ref, y3_ref, acc_ref = scratch
    n, half, box, rows = shape_of(tiles)
    p = pl.program_id(0)
    first = tiles[0] if tables else 0
    columns = slice(tiles[0] * 128, tiles[0] * 128 + n * 128)

    @pl.when(p == 0)
    def _():
        def trig(o, _):
            for r in range(0, NT2, 48):
                h = angle_ref[o, r : r + 48, :] * 0.5
                z = h * h
                s = horner(z, SIN) * h
                c = horner(z, COS)
                cos_ref[o, r : r + 48, :] = 1.0 - 2.0 * (s * s)
                sin_ref[o, r : r + 48, :] = 2.0 * (s * c)
            return 0

        lax.fori_loop(0, 8, trig, 0)
        tt = stencil_t(ti_ref[...], tw_ref[...], 128, even_odd)
        t = jnp.transpose(jnp.concatenate([tt, jnp.zeros((128, 64), F32)], axis=1))[:NT2, :NT1]
        hi, lo = split(t)
        t3_ref[...] = jnp.concatenate([hi, hi, lo], axis=1)
        for ref, shift in ((pe_ref, 0), (po_ref, 64)):
            hi, lo = split(stencil_t(pi_ref[:, columns], pw_ref[:, columns], 256, lambda a: a + shift))
            ref[0], ref[1] = hi, lo

    for k in range(8):
        for part in range(2):
            row = (k * 2 + part) * 48
            for tile in range(3):
                v = x_ref[pl.ds(k * 288 + 2 * tile + part, 48, stride=6), :]
                hi, lo = split(v)
                vh_ref[row : row + 48, tile * 128 : tile * 128 + 128] = hi
                vl_ref[row : row + 48, tile * 128 : tile * 128 + 128] = lo
    for odd, ref in ((0, pe_ref), (1, po_ref)):
        cols = slice(odd * 128, odd * 128 + 256)
        for m in range(0, 768, 192):
            vh, vl = vh_ref[m : m + 192, cols], vl_ref[m : m + 192, cols]
            y = dot(vh, ref[0]) + dot(vl, ref[0]) + dot(vh, ref[1])
            yh, yl = split(y)
            for kk in range(2):
                for part in range(2):
                    r = (kk * 2 + part) * 48
                    for j in range(n):
                        col = j * 256 + part * 128
                        for base, v in ((0, yh), (96, yl)):
                            y3_ref[m // 96 + kk, base + odd * 48 : base + odd * 48 + 48, col : col + 128] = v[
                                r : r + 48, j * 128 : j * 128 + 128
                            ]

    for k in range(8):
        o = oct_ref[p, k]
        for j in range(n):
            y = y3_ref[k, :, j * 256 : j * 256 + 256]
            f = dot(t3_ref[:, :192], y) + dot(t3_ref[:, 192:], y[:96])
            re, im = f[:, :128], f[:, 128:]
            at = (first + j) * 128
            c = cos_ref[o, :, at : at + 128]
            s = sin_ref[o, :, at : at + 128]
            if k == 0:
                acc_ref[2 * j] = re * c - im * s
                acc_ref[2 * j + 1] = re * s + im * c
            else:
                acc_ref[2 * j] += re * c - im * s
                acc_ref[2 * j + 1] += re * s + im * c

    for part in range(2):
        for j in range(n):
            for r in range(3):
                base = p * box + part * half + j * 3 + r
                for zh in range(2):
                    v = acc_ref[2 * j + part, pl.ds(3 * zh + r, 32, stride=6), :]
                    out_ref[pl.ds(zh * 32 * rows + base, 32, stride=rows), :] = v


def operators_kernel(zh_ref, t_ref, first_ref, second_ref):
    half = zh_ref[0] * 18

    def one(d, _):
        for ref, tiles, slot, gap in ((first_ref, FIRST, SLOT, 8), (second_ref, SECOND, SLOT // 2, 3)):
            for part in range(2):
                for jj, j in enumerate(tiles):
                    v = t_ref[pl.ds(d * 36 + half + j * 2 + part, 3, stride=6), :]
                    ref[pl.ds(d * slot + part * gap + jj * 3, 3), :] = v
        return 0

    lax.fori_loop(0, NDISP, one, 0, unroll=4)


def translate_kernel(tiles, src_ref, disp_ref, own_ref, other_ref, t_ref, out_ref, s_ref):
    n, half, box, rows = shape_of(tiles)

    def lay(i, _):
        for first, ref in ((0, own_ref), (CHIPS, other_ref)):
            for p in range(PARENTS):
                re = ref[pl.ds(i * rows + p * box, half), :]
                im = ref[pl.ds(i * rows + p * box + half, half), :]
                to = ((first + i) * PARENTS + p) * 16
                s_ref[pl.ds(to, half), :] = re
                s_ref[pl.ds(to + 8, half), :] = im
                if n == 1:
                    s_ref[pl.ds(to + 3, half), :] = im
                    s_ref[pl.ds(to + 11, half), :] = re
        return 0

    lax.fori_loop(0, CHIPS, lay, 0, unroll=4)

    def receiver(i, _):
        sums = None
        for q in range(NPART):
            a = pl.multiple_of(src_ref.at[pl.ds(q * BOXES, BOXES)][i], 8)
            d = pl.multiple_of(disp_ref.at[pl.ds(q * BOXES, BOXES)][i], 8)
            s0, s1 = s_ref[pl.ds(a, 8), :], s_ref[pl.ds(a + 8, 8), :]
            t0 = t_ref[pl.ds(d, 8), :]
            if n == 1:
                terms = (t0 * s0, t0 * s1)
            else:
                t1 = t_ref[pl.ds(d + 8, 8), :]
                terms = (t0 * s0, t1 * s1, t0 * s1, t1 * s0)
            sums = terms if q == 0 else tuple(x + y for x, y in zip(sums, terms))
        if n == 1:
            re, im = sums[0][0:3] - sums[0][3:6], sums[1][0:3] + sums[1][3:6]
        else:
            re, im = (sums[0] - sums[1])[:half], (sums[2] + sums[3])[:half]
        to = (i // PARENTS) * rows + (i % PARENTS) * box
        out_ref[pl.ds(to, half), :] = re
        out_ref[pl.ds(to + half, half), :] = im
        return 0

    lax.fori_loop(0, CHIPS * PARENTS, receiver, 0, unroll=4)


def disaggregate_kernel(tiles, oct_ref, x_ref, cos_ref, sin_ref, ti_ref, tw_ref, pi_ref, pw_ref, *rest):
    (*before_ref, out_ref, t_ref, pe_ref, po_ref, in_ref, z3_ref) = rest
    n, half, box, rows = shape_of(tiles)
    p = pl.program_id(0)
    columns = slice(tiles[0] * 128, tiles[0] * 128 + n * 128)

    @pl.when(p == 0)
    def _():
        t_ref[...] = jnp.concatenate(split(stencil_t(ti_ref[...], tw_ref[...], NT1, even_odd)), axis=0)
        for ref, shift in ((pe_ref, 0), (po_ref, 64)):
            m = jnp.transpose(stencil_t(pi_ref[:, columns], pw_ref[:, columns], 256, lambda a: a + shift))
            hi, lo = split(m)
            ref[...] = jnp.concatenate([hi, hi, lo], axis=0)

    for part in range(2):
        for j in range(n):
            for r in range(3):
                base = p * box + part * half + j * 3 + r
                for zh in range(2):
                    v = x_ref[pl.ds(zh * 32 * rows + base, 32, stride=rows), :]
                    in_ref[2 * j + part, pl.ds(3 * zh + r, 32, stride=6), :] = v

    for k in range(8):
        o = oct_ref[p, k]
        for j in range(n):
            re, im = in_ref[2 * j], in_ref[2 * j + 1]
            c = cos_ref[o, :, j * 128 : j * 128 + 128]
            s = sin_ref[o, :, j * 128 : j * 128 + 128]
            hi, lo = split(jnp.concatenate([re * c + im * s, im * c - re * s], axis=1))
            g = dot(t_ref[...], hi)
            z = g[:NT1] + g[NT1:] + dot(t_ref[:NT1], lo)
            hi, lo = split(z)
            for part in range(2):
                for odd in range(2):
                    for base, v in ((0, hi), (n * 128, lo), (n * 256, hi)):
                        row = (k * 2 + part) * 48
                        z3_ref[odd, row : row + 48, base + j * 128 : base + j * 128 + 128] = v[
                            odd * 48 : odd * 48 + 48, part * 128 : part * 128 + 128
                        ]

    for first in range(0, 8, 4):
        span = slice(first * 96, first * 96 + 384)
        even = dot(z3_ref[0, span, :], pe_ref[...])
        odd = dot(z3_ref[1, span, :], po_ref[...])
        blocks = (even[:, :128], even[:, 128:] + odd[:, :128], odd[:, 128:])
        for k in range(4):
            for part in range(2):
                at = (k * 2 + part) * 48
                for tile in range(3):
                    to = pl.ds((first + k) * 288 + 2 * tile + part, 48, stride=6)
                    v = blocks[tile][at : at + 48]
                    out_ref[to, :] = v + before_ref[0][to, :] if before_ref else v


def whole(shape):
    return pl.BlockSpec(shape, lambda *_: (0,) * len(shape))


VMEM = pl.BlockSpec(memory_space=pltpu.VMEM)
SMEM = pl.BlockSpec(memory_space=pltpu.SMEM)
STENCILS = [whole((4, NT2)), whole((4, NT2)), whole((4, NP2)), whole((4, NP2))]
PARAMS = pltpu.CompilerParams(vmem_limit_bytes=50 * 2**20)
ROOMY = pltpu.CompilerParams(vmem_limit_bytes=60 * 2**20)
CHILDREN = pl.BlockSpec((8 * 288, 128), lambda p: (p, 0))


def cost(flops, nbytes):
    return pl.CostEstimate(flops=flops, bytes_accessed=nbytes, transcendentals=0)


def table_of(tiles):
    n = len(tiles)
    return pl.BlockSpec((8, NT2, 128 * n), lambda p: (0, 0, tiles[0] // n))


def aggregate(tiles, tables):
    n, _, _, rows = shape_of(tiles)
    table = (8, NT2, NP2)
    part = (8, NT2, 128 * n)
    shapes = [jax.ShapeDtypeStruct((CHIPS * rows, 128), F32)]
    specs = [whole((CHIPS * rows, 128))]
    trig = []
    if tables:
        shapes += [jax.ShapeDtypeStruct(table, F32)] * 2
        specs += [whole(table)] * 2
    else:
        trig = [pltpu.VMEM(part, F32)] * 2
    return pl.pallas_call(
        functools.partial(aggregate_kernel, tiles, tables),
        grid=(PARENTS,),
        in_specs=[SMEM, CHILDREN, whole(table) if tables else table_of(tiles), *STENCILS],
        out_specs=specs,
        out_shape=shapes,
        scratch_shapes=trig
        + [
            pltpu.VMEM((NT2, 288), BF16),
            pltpu.VMEM((2, 256, 128 * n), BF16),
            pltpu.VMEM((2, 256, 128 * n), BF16),
            pltpu.VMEM((768, 384), BF16),
            pltpu.VMEM((768, 384), BF16),
            pltpu.VMEM((8, 192, 256 * n), BF16),
            pltpu.VMEM((2 * n, NT2, 128), F32),
        ],
        compiler_params=ROOMY,
        cost_estimate=cost(n * 4 * 10**9, 10**7),
        name=f"aggregate{n}",
    )


def operators():
    return pl.pallas_call(
        operators_kernel,
        in_specs=[SMEM, VMEM],
        out_specs=[VMEM, VMEM],
        out_shape=[jax.ShapeDtypeStruct((NDISP * slot, 128), F32) for slot in (SLOT, SLOT // 2)],
        compiler_params=ROOMY,
        cost_estimate=cost(10**6, 10**7),
        name="operators",
    )


def translate(tiles):
    n, _, _, rows = shape_of(tiles)
    return pl.pallas_call(
        functools.partial(translate_kernel, tiles),
        in_specs=[SMEM, SMEM, VMEM, VMEM, VMEM],
        out_specs=VMEM,
        out_shape=jax.ShapeDtypeStruct((CHIPS * rows, 128), F32),
        scratch_shapes=[pltpu.VMEM((512 * 16, 128), F32)],
        compiler_params=PARAMS,
        cost_estimate=cost(10**8, 10**7),
        name=f"translate{n}",
    )


def disaggregate(tiles, more):
    n, _, _, rows = shape_of(tiles)
    return pl.pallas_call(
        functools.partial(disaggregate_kernel, tiles),
        grid=(PARENTS,),
        in_specs=[SMEM, whole((CHIPS * rows, 128)), table_of(tiles), table_of(tiles), *STENCILS] + [CHILDREN] * more,
        out_specs=CHILDREN,
        out_shape=jax.ShapeDtypeStruct((32 * 288, 128), F32),
        scratch_shapes=[
            pltpu.VMEM((2 * NT1, NT2), BF16),
            pltpu.VMEM((384 * n, 256), BF16),
            pltpu.VMEM((384 * n, 256), BF16),
            pltpu.VMEM((2 * n, NT2, 128), F32),
            pltpu.VMEM((2, 768, 384 * n), BF16),
        ],
        compiler_params=PARAMS,
        cost_estimate=cost(n * 4 * 10**9, 10**7),
        name=f"disaggregate{n}",
    )


def exchange(a):
    return lax.all_to_all(a.reshape(CHIPS, -1, 128), CHIP, 0, 0, tiled=True).reshape(a.shape)


def together(*arrays):
    return lax.optimization_barrier(arrays)


def local(
    child_out, child_octant, theta_index, theta_weight, phi_index, phi_weight,
    shift_angle, partner_src, partner_disp, translation,
):
    core = lax.axis_index("c")
    zh = lax.axis_index("zh")
    swap = [(0, 1), (1, 0)]
    x = child_out.reshape(32, 2, 144, 128).transpose(0, 2, 1, 3).reshape(32 * 288, 128)
    stencils = (theta_index.T, theta_weight.T, phi_index.T, phi_weight.T)

    def mine(a):
        return lax.dynamic_index_in_dim(a.T.reshape(NPART, 2, 2, 128), core, 2, keepdims=False).reshape(-1)

    src = mine(partner_src)
    holder, p = src // 4, src % 4
    far = jnp.where((holder // 32) % 2 == core, 0, 1)
    src_at = ((far * CHIPS + (holder // 64) * 32 + holder % 32) * PARENTS + p) * SLOT
    disp1 = mine(partner_disp) * SLOT
    disp2 = disp1 // 2
    ops, = together(translation.transpose(0, 2, 1, 3).reshape(NDISP * 6, 2, NP2))
    ops = ops.reshape(NDISP * 6, 2, 3, 128).transpose(0, 2, 1, 3).reshape(NDISP * 36, 128)

    (out1,) = aggregate(FIRST, False)(child_octant, x, shift_angle, *stencils)
    got1 = exchange(out1)
    x2, _ = together(x, out1)
    out2, cosine, sine = aggregate(SECOND, True)(child_octant, x2, shift_angle, *stencils)
    ops1, ops2 = operators()(zh.reshape(1), ops)
    got1, out2, ops1, ops2, src_at, disp1, disp2 = together(got1, out2, ops1, ops2, src_at, disp1, disp2)

    got2 = exchange(out2)
    other1 = lax.ppermute(got1, "c", swap)
    in1 = translate(FIRST)(src_at, disp1, got1, other1, ops1)
    in1, got2 = together(in1, got2)

    back1 = exchange(in1)
    other2 = lax.ppermute(got2, "c", swap)
    in2 = translate(SECOND)(src_at, disp2, got2, other2, ops2)
    in2, back1 = together(in2, back1)

    back2 = exchange(in2)
    y = disaggregate(FIRST, 0)(child_octant, back1, cosine, sine, *stencils)
    y, back2 = together(y, back2)
    y = disaggregate(SECOND, 1)(child_octant, back2, cosine, sine, *stencils, y)
    return y.reshape(32, 144, 2, 128).transpose(0, 2, 1, 3).reshape(32, 2, NT1 * NP1)


def solution(mesh):
    fine = Mesh(mesh.devices.reshape(2, 2, 2, 4, 4), ALL)
    boxes = P(ALL)
    in_specs = (boxes, boxes, P(), P(), P(), P(), P(), P(), P(), P(None, None, ("zl", "y", "x"), None))
    return jax.shard_map(local, mesh=fine, in_specs=in_specs, out_specs=boxes, check_vma=False)
```
